128 devices in a mesh: depth: 16 (over z, y_lo, core), height: 8 (over x, y_hi).
Axes of the slice: x: 4, y: 4 (y_hi: 2, y_lo: 2; y = y_hi * 2 + y_lo), z: 4, core: 2. Of those that a mesh axis runs over, the one named last changes fastest.
Arguments:
- volume: bfloat16 [16, 256, 64, 256], P(None, 'depth', 'height'), may hold values from -6 to 6
- kernel: bfloat16 [3, 3, 32, 48], replicated, may hold values from -0.3125 to 0.3125
- conv_bias: float32 [32], replicated, may hold values from -3 to 3
- cotangent: bfloat16 [32, 128, 32, 128], P(None, 'depth', 'height'), may hold values from -6 to 6
Outputs:
- pooled: bfloat16 [32, 128, 32, 128], P(None, ('depth', 'height'))
- grad_volume: bfloat16 [16, 256, 64, 256], P(None, 'depth', 'height')
- grad_kernel: float32 [3, 3, 32, 48], replicated
- grad_bias: float32 [32], replicated
The draws below stay inside these ranges and needn't reach their ends.
All inputs are finite; a program needn't handle non-finite values.
Results may differ from the reference program's by a relative error of at most 0.005.
Values may be sent and summed in bfloat16 or wider, within the bound.
A program may use at most 128 MiB of HBM per device.

```python
import jax
import jax.numpy as jnp
from jax import lax

CIN = 16
COUT = 32
W = 256
DEPTH = 256
HEIGHT = 64
VOLUME = 4194304


def steps_of(key, shape, shards, low, high):
    loudness = 1.0
    for axis_at, blocks in shards:
        draws = jax.random.uniform(jax.random.fold_in(jax.random.fold_in(key, 6), axis_at), (blocks,), jnp.float32, low / len(shards), high / len(shards))
        loudness = loudness * jnp.repeat(jnp.exp(draws), shape[axis_at] // blocks).reshape((-1,) + (1,) * (len(shape) - 1 - axis_at))
    return loudness


def scatter_about(stream_key, dims, scale, most, shards=(), held_as=jnp.bfloat16):
    values = scale * jax.random.normal(stream_key, dims, jnp.float32)
    if shards:
        values = values * steps_of(stream_key, dims, shards, -0.22, 0.18)
    return jnp.clip(values, -most, most).astype(held_as)


def setup_inputs(seed: int = 0) -> dict:
    streams_of = jax.random.split(jax.random.key(seed), 5)
    return {
        "volume": scatter_about(streams_of[0], (CIN, DEPTH, HEIGHT, W), 1.0, 6.0, ((1, 16), (2, 8))),
        "kernel": scatter_about(streams_of[1], (3, 3, COUT, 3 * CIN), (27 * CIN) ** -0.5, 0.3125),
        "conv_bias": scatter_about(streams_of[2], (COUT,), 0.5, 3.0, (), jnp.float32),
        "cotangent": scatter_about(streams_of[3], (COUT, DEPTH // 2, HEIGHT // 2, W // 2), 1.0, 6.0, ((1, 16), (2, 8))),
    }


leak_rate = 0.3

def smooth_leaky(values):
    return leak_rate * values + (1.0 - leak_rate) * jax.nn.softplus(values)

def leaky_slope(values):
    return leak_rate + (1.0 - leak_rate) * jax.nn.sigmoid(values)

def correlate(volume_data, kernel_data):
    filters = kernel_data.reshape(3, 3, COUT, 3, CIN).transpose(2, 4, 0, 1, 3)
    result = lax.conv_general_dilated(volume_data[None], filters, (1, 1, 1), ((1, 1), (1, 1), (1, 1)), precision=lax.Precision.HIGHEST)
    return result[0]

def pool_cells(tensor):
    channels, depth_n, height_n, width_n = tensor.shape
    return tensor.reshape(channels, depth_n // 2, 2, height_n // 2, 2, width_n // 2, 2).mean(axis=(2, 4, 6))

def spread_cells(tensor):
    channels, depth_n, height_n, width_n = tensor.shape
    enlarged = jnp.broadcast_to(tensor[:, :, None, :, None, :, None], (channels, depth_n, 2, height_n, 2, width_n, 2))
    return enlarged.reshape(channels, 2 * depth_n, 2 * height_n, 2 * width_n)

def reference(volume, kernel, conv_bias, cotangent):
    volume_wide = volume.astype(jnp.float32)
    kernel_wide = kernel.astype(jnp.float32)
    linear, pullback = jax.vjp(correlate, volume_wide, kernel_wide)
    before = linear + conv_bias.astype(jnp.float32)[:, None, None, None]
    pooled = pool_cells(smooth_leaky(before)).astype(jnp.bfloat16)
    upward = spread_cells(cotangent.astype(jnp.float32)) * 0.125
    local_grad = (upward * leaky_slope(before)).astype(jnp.bfloat16)
    grad_wide = local_grad.astype(jnp.float32)
    grad_volume, grad_kernel = pullback(grad_wide)
    norm_factor = 1.0 / jnp.sqrt(jnp.float32(VOLUME))
    grad_bias = lax.optimization_barrier(jnp.sum(grad_wide, axis=(1, 2, 3))) * norm_factor
    return (pooled, grad_volume.astype(jnp.bfloat16), grad_kernel * norm_factor, grad_bias)
```

```python
import functools
import math

import jax
import jax.numpy as jnp
from jax import lax
from jax.experimental import pallas as pl
from jax.experimental.pallas import tpu as pltpu
from jax.sharding import PartitionSpec as P

BF = jnp.bfloat16
F32 = jnp.float32
MESH = pl.DeviceIdType.MESH

CI, CO, ND, NH, W = 16, 32, 16, 8, 256
ROWS = CO * NH
XROWS = CI * NH
KS = 512
ONES = 480
PAIRS = ND // 2


def dot(a, b):
    return jnp.dot(a, b, preferred_element_type=F32)


def dot_nt(a, b):
    return lax.dot_general(a, b, (((1,), (1,)), ((), ())), preferred_element_type=F32)


def iota(shape, dim):
    return lax.broadcasted_iota(jnp.int32, shape, dim)


def one_hot(cond, value=1.0):
    return jnp.where(cond, value, 0.0).astype(BF)


def shift_right(x):
    rolled = pltpu.roll(x, 1, 1)
    return jnp.where(iota(x.shape, 1) == 0, jnp.zeros_like(x), rolled)


def shift_left(x):
    rolled = pltpu.roll(x, x.shape[1] - 1, 1)
    return jnp.where(iota(x.shape, 1) == x.shape[1] - 1, jnp.zeros_like(x), rolled)


def kernel_body(nd, nh, vol, ker, bias, cot, pooled, gvol, gker, gbias,
                xa, ga, tm, tb, acc, om, um, hs, rh, rd, ps, rpool, ph, rp, rpc, pd, rpd, comp, rs, rs2, piece,
                full, s_v, r_v, s_p, r_p, s_g, r_g, s_a, r_a, s_b, r_b, s_c, r_c):
    i = lax.axis_index("depth")
    j = lax.axis_index("height")
    up_i, dn_i = lax.rem(i + 1, nd), lax.rem(i + nd - 1, nd)
    up_j, dn_j = lax.rem(j + 1, nh), lax.rem(j + nh - 1, nh)
    first_i, last_i = i == 0, i == nd - 1
    first_j, last_j = j == 0, j == nh - 1

    barrier = pltpu.get_barrier_semaphore()

    def greet_depth(k, carry):
        pl.semaphore_signal(barrier, inc=1, device_id=(lax.rem(i + k, nd), j), device_id_type=MESH)
        return carry

    def greet_height(k, carry):
        pl.semaphore_signal(barrier, inc=1, device_id=(i, lax.rem(j + k, nh)), device_id_type=MESH)
        return carry

    lax.fori_loop(1, nd, greet_depth, 0)
    lax.fori_loop(1, nh, greet_height, 0)
    for di in (dn_i, up_i):
        for dj in (dn_j, up_j):
            pl.semaphore_signal(barrier, inc=1, device_id=(di, dj), device_id_type=MESH)

    row, col = iota((2 * CI, XROWS), 0), iota((2 * CI, XROWS), 1)
    edge_rows = one_hot(col == (row % CI) * NH + (row // CI) * (NH - 1))
    for d in range(ND):
        x = vol[:, d].reshape(XROWS, W)
        edge = dot(edge_rows, x).astype(BF)
        hs[0, d] = edge[:CI]
        hs[1, d] = edge[CI:]

    pl.semaphore_wait(barrier, nd - 1 + nh - 1 + 4)

    def remote(src, dst, send, recv, target):
        return pltpu.make_async_remote_copy(
            src_ref=src, dst_ref=dst, send_sem=send, recv_sem=recv, device_id=target, device_id_type=MESH)

    vol_copies = [
        remote(hs.at[0], rh.at[1, pl.ds(1, ND)], s_v.at[0], r_v.at[0], (i, dn_j)),
        remote(hs.at[1], rh.at[0, pl.ds(1, ND)], s_v.at[1], r_v.at[1], (i, up_j)),
        remote(vol.at[:, 0], rd.at[1], s_v.at[2], r_v.at[2], (dn_i, j)),
        remote(vol.at[:, ND - 1], rd.at[0], s_v.at[3], r_v.at[3], (up_i, j)),
        remote(hs.at[0, 0], rh.at[1, ND + 1], s_v.at[4], r_v.at[4], (dn_i, dn_j)),
        remote(hs.at[0, ND - 1], rh.at[1, 0], s_v.at[5], r_v.at[5], (up_i, dn_j)),
        remote(hs.at[1, 0], rh.at[0, ND + 1], s_v.at[6], r_v.at[6], (dn_i, up_j)),
        remote(hs.at[1, ND - 1], rh.at[0, 0], s_v.at[7], r_v.at[7], (up_i, up_j)),
    ]
    for copy in vol_copies:
        copy.start()

    def put_slab(p, x):
        xa[p, 0:XROWS] = shift_right(x)
        xa[p, XROWS:2 * XROWS] = x
        xa[p, 2 * XROWS:3 * XROWS] = shift_left(x)

    for d in range(ND):
        put_slab(d + 1, vol[:, d].reshape(XROWS, W))

    row, col = iota((3 * CI, 640), 0), iota((3 * CI, 640), 1)
    expand = one_hot(((col < 384) & (row == col // NH))
                     | ((col >= 384) & (col < 512) & (row == col - 384))
                     | ((col >= 512) & (row + 3 * CI == col - 512)))
    lane_h = iota((CO, 384), 1) % NH
    for a in range(3):
        taps = dot(ker[a], expand)
        for h in range(NH):
            band = jnp.zeros((CO, 384), F32)
            for b in range(3):
                if 0 <= h + b - 1 < NH:
                    band = jnp.where(lane_h == h + b - 1, taps[b * CO:(b + 1) * CO, :384], band)
            tm[h * CO:(h + 1) * CO, a * KS:a * KS + 384] = band.astype(BF)
            if h == 0:
                side = taps[0:CO, 384:512].astype(BF)
            elif h == NH - 1:
                side = taps[2 * CO:3 * CO, 512:640].astype(BF)
            else:
                side = jnp.zeros((CO, 128), BF)
            tm[h * CO:(h + 1) * CO, a * KS + 384:(a + 1) * KS] = side
    for a in range(3):
        flipped = tm[:, a * KS:(a + 1) * KS].T
        for e in range(3):
            at = (2 - a) * 3 * ROWS + e * ROWS
            tb[0:XROWS, at:at + ROWS] = flipped[e * XROWS:(e + 1) * XROWS]
            tb[XROWS:XROWS + CI, at:at + ROWS] = flipped[384 + e * CI:384 + (e + 1) * CI]
            tb[XROWS + CI:XROWS + 2 * CI, at:at + ROWS] = flipped[432 + e * CI:432 + (e + 1) * CI]

    row, col = iota((128, 128), 0), iota((128, 128), 1)
    to_h_major = one_hot(col == (row % CO) * 4 + row // CO)
    to_o_major = one_hot(col == (row % 4) * CO + row // 4)
    spread = one_hot(iota((128, W), 0) == iota((128, W), 1) // 2)
    gather = one_hot((iota((2 * W, 128), 0) % W) // 2 == iota((2 * W, 128), 1), 0.125)
    for q in range(PAIRS):
        ct = cot[:, q].reshape(128, 128)
        um[q] = dot(dot(to_h_major, ct).astype(BF), spread)
    eye = iota((CO, CO), 0) == iota((CO, CO), 1)
    bias_col = jnp.sum(jnp.where(eye, jnp.broadcast_to(bias[...], (CO, CO)), 0.0), axis=1, keepdims=True)
    bias_rows = jnp.concatenate([bias_col] * NH, axis=0)

    ones_rows = one_hot(iota((KS - ONES, W), 0) == 0)
    for p in range(ND + 2):
        xa[p, ONES:KS] = ones_rows

    for copy in vol_copies:
        copy.wait_recv()
    zero_slab = jnp.zeros((XROWS, W), BF)
    put_slab(0, jnp.where(first_i, zero_slab, rd[0].reshape(XROWS, W)))
    put_slab(ND + 1, jnp.where(last_i, zero_slab, rd[1].reshape(XROWS, W)))
    for side in range(2):
        for p in range(ND + 2):
            outside = first_j if side == 0 else last_j
            if p == 0:
                outside = outside | first_i
            if p == ND + 1:
                outside = outside | last_i
            x = jnp.where(outside, jnp.zeros((CI, W), BF), rh[side, p])
            at = 384 + side * 48
            xa[p, at:at + CI] = shift_right(x)
            xa[p, at + CI:at + 2 * CI] = x
            xa[p, at + 2 * CI:at + 3 * CI] = shift_left(x)

    def forward(q, carry):
        cells = None
        for k in range(2):
            d = 2 * q + k
            before = dot(tm[...], xa[pl.ds(d, 3)].reshape(3 * KS, W)) + bias_rows
            th = jnp.tanh(0.5 * before)
            act = jnp.maximum(before, 0.3 * before) - 0.7 * jnp.log(0.5 + 0.5 * jnp.abs(th))
            slope = (0.08125 + 0.04375 * th).reshape(4, 2, CO, W)
            g = (um[q].reshape(4, 1, CO, W) * slope).reshape(ROWS, W).astype(BF)
            ga[d, 0:ROWS] = shift_left(g)
            ga[d, ROWS:2 * ROWS] = g
            ga[d, 2 * ROWS:3 * ROWS] = shift_right(g)
            part = act.reshape(4, 2, CO, W).sum(axis=1).reshape(128, W)
            cells = part if cells is None else cells + part
        high = cells.astype(BF)
        low = (cells - high.astype(F32)).astype(BF)
        mean = dot(jnp.concatenate([high, low], axis=1), gather).astype(BF)
        ps[q] = dot(to_o_major, mean).astype(BF).reshape(CO, 4, 128)
        return carry

    lax.fori_loop(0, PAIRS, forward, 0)

    def pool_copy(k):
        t = lax.rem(j + k, nh)
        return remote(ps.at[t], rpool.at[j], s_p.at[k], r_p.at[k], (i, t))

    def pool_start(k, carry):
        pool_copy(k).start()
        return carry

    lax.fori_loop(1, nh, pool_start, 0)
    rpool[j] = ps[j]

    acc[...] = jnp.zeros_like(acc)

    def taps_grad(q, carry):
        d = 4 * q
        left = jnp.concatenate([xa[pl.ds(d + k, 3)].reshape(3 * KS, W) for k in range(4)], axis=1)
        right = jnp.concatenate([ga[d + k, ROWS:2 * ROWS] for k in range(4)], axis=1)
        acc[...] += dot_nt(left, right)
        return carry

    lax.fori_loop(0, ND // 4, taps_grad, 0)

    sub, lane_at = iota((1, NH, W), 1), iota((1, NH, W), 2) // CO
    half_at = iota((48, W), 1) // CO
    lane_block = iota((48, 128), 1) // CO

    def fold(x):
        x = x[:, :128] + x[:, 128:]
        x = x + pltpu.roll(x, 64, 1)
        return x + pltpu.roll(x, 32, 1)

    comp[...] = jnp.zeros_like(comp)
    for a in range(3):
        own = acc[a * KS:a * KS + 384].reshape(48, NH, W)
        for b in range(3):
            t = a * 3 + b
            diag = jnp.sum(jnp.where(sub == lane_at + (b - 1), own, 0.0), axis=1)
            if b == 0:
                diag = diag + jnp.where(half_at == 0, acc[a * KS + 384:a * KS + 432], 0.0)
            if b == 2:
                diag = diag + jnp.where(half_at == NH - 1, acc[a * KS + 432:a * KS + 480], 0.0)
            diag = fold(diag)
            if t < 8:
                at = (t % 2) * 48
                comp[at:at + 48] += jnp.where(lane_block == t // 2, diag, 0.0)
            else:
                comp[96:128] += jnp.where(lane_block[:32] == 0, diag[:32], 0.0)
                comp[96:112] += jnp.where(lane_block[:16] == 1, diag[32:48], 0.0)
    comp[96:104] += jnp.where(lane_block[:8] == 2, fold(acc[KS + ONES:KS + ONES + 8]), 0.0)

    rows = 128 // nd

    def scatter_copy(k):
        t = lax.rem(i + k, nd)
        return remote(comp.at[pl.ds(pl.multiple_of(t * rows, rows), rows)], rs.at[i], s_a.at[k], r_a.at[k], (t, j))

    def all_copy(k):
        t = lax.rem(j + k, nh)
        return remote(piece, rs2.at[j], s_b.at[k], r_b.at[k], (i, t))

    def gather_copy(k):
        t = lax.rem(i + k, nd)
        here = full.at[pl.ds(pl.multiple_of(i * rows, rows), rows)]
        return remote(here, here, s_c.at[k], r_c.at[k], (t, j))

    def run(count, make, act):
        def step(k, carry):
            getattr(make(k), act)()
            return carry
        lax.fori_loop(1, count, step, 0)

    run(nd, scatter_copy, "start")
    rs[i] = comp[pl.ds(pl.multiple_of(i * rows, rows), rows)]

    def back(lo, hi, d):
        k0 = (lo - d + 1) * 3 * ROWS
        n = hi - lo
        return dot(tb[:, k0:k0 + n * 3 * ROWS], ga[lo:hi].reshape(n * 3 * ROWS, W))

    def keep(d, out):
        ph[0, d + 1] = out[XROWS:XROWS + CI].astype(BF)
        ph[1, d + 1] = out[XROWS + CI:].astype(BF)

    for side, d in ((0, -1), (1, ND)):
        out = back(max(d - 1, 0), min(d + 2, ND), d)
        pd[side] = out[:XROWS].astype(BF)
        keep(d, out)
    grad_copies = [
        remote(pd.at[0], rpd.at[1], s_g.at[0], r_g.at[0], (dn_i, j)),
        remote(pd.at[1], rpd.at[0], s_g.at[1], r_g.at[1], (up_i, j)),
        remote(ph.at[0, 0], rpc.at[1, 1], s_g.at[2], r_g.at[2], (dn_i, dn_j)),
        remote(ph.at[1, 0], rpc.at[1, 0], s_g.at[3], r_g.at[3], (dn_i, up_j)),
        remote(ph.at[0, ND + 1], rpc.at[0, 1], s_g.at[4], r_g.at[4], (up_i, dn_j)),
        remote(ph.at[1, ND + 1], rpc.at[0, 0], s_g.at[5], r_g.at[5], (up_i, up_j)),
    ]
    for copy in grad_copies:
        copy.start()

    def send_rows(n):
        part = pl.ds(1 + 4 * n, 4)
        for side, t in ((0, dn_j), (1, up_j)):
            at = 6 + 2 * n + side
            copy = remote(ph.at[side, part], rp.at[1 - side, pl.ds(4 * n, 4)], s_g.at[at], r_g.at[at], (i, t))
            copy.start()
            grad_copies.append(copy)

    for d in (0, ND - 1):
        out = back(max(d - 1, 0), min(d + 2, ND), d)
        om[d] = out[:XROWS]
        keep(d, out)

    def inner(d):
        out = dot(tb[...], ga[pl.ds(d - 1, 3)].reshape(9 * ROWS, W))
        om[d] = out[:XROWS]
        ph[0, d + 1] = out[XROWS:XROWS + CI].astype(BF)
        ph[1, d + 1] = out[XROWS + CI:].astype(BF)

    for d in (1, 2, 3):
        inner(d)
    send_rows(0)
    for d in (4, 5, 6, 7):
        inner(d)
    send_rows(1)

    run(nd, scatter_copy, "wait_recv")
    total = rs[0]
    for k in range(1, nd):
        total = total + rs[k]
    piece[...] = total
    rs2[j] = total
    run(nh, all_copy, "start")

    for d in (8, 9, 10, 11):
        inner(d)
    send_rows(2)
    for d in (12, 13, 14):
        inner(d)
    send_rows(3)

    run(nh, all_copy, "wait_recv")
    total = rs2[0]
    for k in range(1, nh):
        total = total + rs2[k]
    full[pl.ds(pl.multiple_of(i * rows, rows), rows)] = total
    run(nd, gather_copy, "start")

    run(nh, pool_copy, "wait_recv")
    for o in range(CO):
        pooled[o, 0] = rpool[:, o].reshape(4 * nh, 128)

    for copy in grad_copies:
        copy.wait_recv()
    row, col = iota((XROWS, 2 * CI), 0), iota((XROWS, 2 * CI), 1)
    place = one_hot(row == (col % CI) * NH + (col // CI) * (NH - 1))
    zero_rows = jnp.zeros((CI, W), BF)

    def edges(low, high, none):
        return dot(place, jnp.concatenate([jnp.where(first_j | none, zero_rows, low),
                                           jnp.where(last_j | none, zero_rows, high)], axis=0))

    for d in range(ND):
        out = om[d] + edges(rp[0, d], rp[1, d], False)
        if d in (0, ND - 1):
            side = 0 if d == 0 else 1
            none = first_i if d == 0 else last_i
            out = out + edges(rpc[side, 0], rpc[side, 1], none)
            out = out + jnp.where(none, zero_slab, rpd[side]).astype(F32)
        gvol[:, d] = out.astype(BF).reshape(CI, NH, W)

    run(nd, gather_copy, "wait_recv")
    norm = 1.0 / math.sqrt(float(ND * NH * W * nd * nh))
    final = full[...] * norm
    turned = final.T
    for t in range(8):
        gker[t // 3, t % 3] = turned[(t // 2) * CO:(t // 2 + 1) * CO, (t % 2) * 48:(t % 2 + 1) * 48]
    gker[2, 2, :, 0:32] = turned[0:CO, 96:128]
    gker[2, 2, :, 32:48] = turned[CO:2 * CO, 96:112]
    gbias[...] = final[96:97, 2 * CO:3 * CO]

    for copy in vol_copies + grad_copies:
        copy.wait_send()
    run(nh, pool_copy, "wait_send")
    run(nd, scatter_copy, "wait_send")
    run(nh, all_copy, "wait_send")
    run(nd, gather_copy, "wait_send")


def shards(nd, nh, volume, kernel, conv_bias, cotangent):
    vmem = pl.BlockSpec(memory_space=pltpu.VMEM)
    rows = 128 // nd
    dma = pltpu.SemaphoreType.DMA
    pooled, gvol, gker, gbias = pl.pallas_call(
        functools.partial(kernel_body, nd, nh),
        out_shape=(
            jax.ShapeDtypeStruct((CO, 1, 4 * nh, 128), BF),
            jax.ShapeDtypeStruct((CI, ND, NH, W), BF),
            jax.ShapeDtypeStruct((3, 3, CO, 3 * CI), F32),
            jax.ShapeDtypeStruct((1, CO), F32),
        ),
        in_specs=[vmem] * 4,
        out_specs=(vmem,) * 4,
        scratch_shapes=[
            pltpu.VMEM((ND + 2, KS, W), BF),
            pltpu.VMEM((ND, 3 * ROWS, W), BF),
            pltpu.VMEM((ROWS, 3 * KS), BF),
            pltpu.VMEM((XROWS + 2 * CI, 9 * ROWS), BF),
            pltpu.VMEM((3 * KS, ROWS), F32),
            pltpu.VMEM((ND, XROWS, W), F32),
            pltpu.VMEM((PAIRS, 128, W), F32),
            pltpu.VMEM((2, ND, CI, W), BF),
            pltpu.VMEM((2, ND + 2, CI, W), BF),
            pltpu.VMEM((2, CI, NH, W), BF),
            pltpu.VMEM((PAIRS, CO, 4, 128), BF),
            pltpu.VMEM((PAIRS, CO, 4, 128), BF),
            pltpu.VMEM((2, ND + 2, CI, W), BF),
            pltpu.VMEM((2, ND, CI, W), BF),
            pltpu.VMEM((2, 2, CI, W), BF),
            pltpu.VMEM((2, XROWS, W), BF),
            pltpu.VMEM((2, XROWS, W), BF),
            pltpu.VMEM((128, 128), F32),
            pltpu.VMEM((nd, rows, 128), F32),
            pltpu.VMEM((nh, rows, 128), F32),
            pltpu.VMEM((rows, 128), F32),
            pltpu.VMEM((128, 128), F32),
            dma((8,)), dma((8,)),
            dma((nh,)), dma((nh,)),
            dma((14,)), dma((14,)),
            dma((nd,)), dma((nd,)),
            dma((nh,)), dma((nh,)),
            dma((nd,)), dma((nd,)),
        ],
        compiler_params=pltpu.CompilerParams(
            collective_id=0, has_side_effects=True, vmem_limit_bytes=56 * 2**20),
        cost_estimate=pl.CostEstimate(flops=10 * 10**9, bytes_accessed=3 * 2**20, transcendentals=2 * 2**20),
        name="conv_step",
    )(volume, kernel.reshape(3, 3 * CO, 3 * CI), conv_bias.reshape(1, CO), cotangent)
    return pooled, gvol, gker, gbias.reshape(CO)


def solution(mesh):
    nd, nh = mesh.shape["depth"], mesh.shape["height"]
    in_specs = (P(None, "depth", "height", None), P(), P(), P(None, "depth", "height", None))
    out_specs = (
        P(None, ("depth", "height"), None, None),
        P(None, "depth", "height", None),
        P(),
        P(),
    )
    return jax.shard_map(
        functools.partial(shards, nd, nh), mesh=mesh, in_specs=in_specs, out_specs=out_specs, check_vma=False)
```

```python
import functools
import math

import jax
import jax.numpy as jnp
from jax import lax
from jax.experimental import pallas as pl
from jax.experimental.pallas import tpu as pltpu
from jax.sharding import PartitionSpec as P

BF = jnp.bfloat16
F32 = jnp.float32
MESH = pl.DeviceIdType.MESH

CI, CO, ND, NH, W = 16, 32, 16, 8, 256
ROWS = CO * NH
XROWS = CI * NH
KM = 3 * XROWS
ONES = 96
PAIRS = ND // 2
RING = 4
NEAR = 8
FAR = RING * RING
PIECE = 128 // NEAR


def dot(a, b):
    return jnp.dot(a, b, preferred_element_type=F32)


def dot_nt(a, b):
    return lax.dot_general(a, b, (((1,), (1,)), ((), ())), preferred_element_type=F32)


def iota(shape, dim):
    return lax.broadcasted_iota(jnp.int32, shape, dim)


def one_hot(cond, value=1.0):
    return jnp.where(cond, value, 0.0).astype(BF)


def shift_right(x):
    rolled = pltpu.roll(x, 1, 1)
    return jnp.where(iota(x.shape, 1) == 0, jnp.zeros_like(x), rolled)


def shift_left(x):
    rolled = pltpu.roll(x, x.shape[1] - 1, 1)
    return jnp.where(iota(x.shape, 1) == x.shape[1] - 1, jnp.zeros_like(x), rolled)


def kernel_body(nd, nh, vol_in, ker, bias, cot_in, pooled, gvol, gker, gbias,
                vol, cot, xa, xh, ga, tm, th, tb, acc, bm, om, um, cells, hs, rh, rd, ps, rpool, ph, rp, rpc, pd, rpd, comp, rs, rs2, piece,
                full, s_in, s_v, r_v, s_p, r_p, s_g, r_g, s_a, r_a, s_b, r_b, s_c, r_c):
    i = lax.axis_index("depth")
    j = lax.axis_index("height")
    up_i, dn_i = lax.rem(i + 1, nd), lax.rem(i + nd - 1, nd)
    up_j, dn_j = lax.rem(j + 1, nh), lax.rem(j + nh - 1, nh)
    first_i, last_i = i == 0, i == nd - 1
    first_j, last_j = j == 0, j == nh - 1
    near = lax.rem(j, 2) * 4 + lax.rem(i, 4)
    far = (i // 4) * RING + j // 2

    def near_target(k):
        t = lax.rem(near + k, NEAR)
        return t, ((i // 4) * 4 + lax.rem(t, 4), (j // 2) * 2 + t // 4)

    def far_target(k):
        t = lax.rem(far + k, FAR)
        return t, ((t // RING) * 4 + lax.rem(i, 4), lax.rem(t, RING) * 2 + lax.rem(j, 2))

    def high_target(k):
        t = lax.rem(j + k, nh)
        return t, (i, t)

    vol_load = pltpu.make_async_copy(vol_in, vol, s_in.at[0])
    cot_load = pltpu.make_async_copy(cot_in, cot, s_in.at[1])
    vol_load.start()
    cot_load.start()
    barrier = pltpu.get_barrier_semaphore()

    def greet(target):
        pl.semaphore_signal(barrier, inc=1, device_id=target, device_id_type=MESH)

    def greet_all(count, make):
        def step(k, carry):
            greet(make(k)[1])
            return carry
        lax.fori_loop(1, count, step, 0)

    for di in (dn_i, up_i):
        for dj in (dn_j, j, up_j):
            greet((di, dj))
    greet_all(nh, high_target)
    greet_all(NEAR, near_target)
    greet_all(FAR, far_target)

    row, col = iota((2 * CI, XROWS), 0), iota((2 * CI, XROWS), 1)
    edge_rows = one_hot(col == (row % CI) * NH + (row // CI) * (NH - 1))
    vol_load.wait()
    for d in range(ND):
        edge = dot(edge_rows, vol[:, d].reshape(XROWS, W)).astype(BF)
        hs[0, d] = edge[:CI]
        hs[1, d] = edge[CI:]

    pl.semaphore_wait(barrier, 6 + nh - 1 + NEAR - 1 + FAR - 1)

    def remote(src, dst, send, recv, target):
        return pltpu.make_async_remote_copy(
            src_ref=src, dst_ref=dst, send_sem=send, recv_sem=recv, device_id=target, device_id_type=MESH)

    vol_copies = [
        remote(vol.at[:, 0], rd.at[1], s_v.at[0], r_v.at[0], (dn_i, j)),
        remote(vol.at[:, ND - 1], rd.at[0], s_v.at[1], r_v.at[1], (up_i, j)),
        remote(hs.at[0, 0], rh.at[1, ND + 1], s_v.at[2], r_v.at[2], (dn_i, dn_j)),
        remote(hs.at[0, ND - 1], rh.at[1, 0], s_v.at[3], r_v.at[3], (up_i, dn_j)),
        remote(hs.at[1, 0], rh.at[0, ND + 1], s_v.at[4], r_v.at[4], (dn_i, up_j)),
        remote(hs.at[1, ND - 1], rh.at[0, 0], s_v.at[5], r_v.at[5], (up_i, up_j)),
        remote(hs.at[0], rh.at[1, pl.ds(1, ND)], s_v.at[6], r_v.at[6], (i, dn_j)),
        remote(hs.at[1], rh.at[0, pl.ds(1, ND)], s_v.at[7], r_v.at[7], (i, up_j)),
    ]
    for copy in vol_copies:
        copy.start()

    def put_slab(p, x):
        xa[p, 0:XROWS] = shift_right(x)
        xa[p, XROWS:2 * XROWS] = x
        xa[p, 2 * XROWS:3 * XROWS] = shift_left(x)

    for d in range(ND):
        put_slab(d + 1, vol[:, d].reshape(XROWS, W))

    row, col = iota((3 * CI, 640), 0), iota((3 * CI, 640), 1)
    expand = one_hot(((col < 384) & (row == col // NH))
                     | ((col >= 384) & (col < 512) & (row == col - 384))
                     | ((col >= 512) & (row + 3 * CI == col - 512)))
    lane_h = iota((CO, 384), 1) % NH
    for a in range(3):
        taps = dot(ker[a], expand)
        for h in range(NH):
            band = jnp.zeros((CO, 384), F32)
            for b in range(3):
                if 0 <= h + b - 1 < NH:
                    band = jnp.where(lane_h == h + b - 1, taps[b * CO:(b + 1) * CO, :384], band)
            tm[h * CO:(h + 1) * CO, a * KM:(a + 1) * KM] = band.astype(BF)
        th[0:CO, a * 128:(a + 1) * 128] = taps[0:CO, 384:512].astype(BF)
        th[CO:2 * CO, a * 128:(a + 1) * 128] = taps[2 * CO:3 * CO, 512:640].astype(BF)

    def own_part(d):
        lo, hi = max(d, 1), min(d + 3, ND + 1)
        k0 = (lo - d) * KM
        bm[d] = dot(tm[:, k0:k0 + (hi - lo) * KM], xa[lo:hi].reshape((hi - lo) * KM, W))

    def own_parts(n, carry):
        for k in range(7):
            d = 1 + 7 * n + k
            bm[d] = dot(tm[...], xa[pl.ds(d, 3)].reshape(3 * KM, W))
        return carry

    lax.fori_loop(0, 2, own_parts, 0)
    own_part(0)
    own_part(ND - 1)

    row, col = iota((128, 128), 0), iota((128, 128), 1)
    to_h_major = one_hot(col == (row % CO) * 4 + row // CO)
    to_o_major = one_hot(col == (row % 4) * CO + row // 4)
    spread = one_hot(iota((128, W), 0) == iota((128, W), 1) // 2)
    gather = one_hot((iota((2 * W, 128), 0) % W) // 2 == iota((2 * W, 128), 1), 0.125)
    cot_load.wait()
    for q in range(PAIRS):
        ct = cot[:, q].reshape(128, 128)
        um[q] = dot(dot(to_h_major, ct).astype(BF), spread)
    eye = iota((CO, CO), 0) == iota((CO, CO), 1)
    bias_col = jnp.sum(jnp.where(eye, jnp.broadcast_to(bias[...], (CO, CO)), 0.0), axis=1, keepdims=True)
    bias_rows = jnp.concatenate([bias_col] * NH, axis=0)

    ones_rows = one_hot(iota((128 - ONES, W), 0) == 0)
    for p in range(ND + 2):
        xh[p, ONES:128] = ones_rows

    for a in range(3):
        flipped = tm[:, a * KM:(a + 1) * KM].T
        side = jnp.concatenate([th[0:CO, a * 128:(a + 1) * 128], jnp.zeros((ROWS - 2 * CO, 128), BF),
                                th[CO:2 * CO, a * 128:(a + 1) * 128]], axis=0).T
        for e in range(3):
            at = (2 - a) * 3 * ROWS + e * ROWS
            tb[0:XROWS, at:at + ROWS] = flipped[e * XROWS:(e + 1) * XROWS]
            tb[XROWS:XROWS + CI, at:at + ROWS] = side[e * CI:(e + 1) * CI]
            tb[XROWS + CI:XROWS + 2 * CI, at:at + ROWS] = side[48 + e * CI:48 + (e + 1) * CI]

    for copy in vol_copies:
        copy.wait_recv()
    zero_slab = jnp.zeros((XROWS, W), BF)
    put_slab(0, jnp.where(first_i, zero_slab, rd[0].reshape(XROWS, W)))
    put_slab(ND + 1, jnp.where(last_i, zero_slab, rd[1].reshape(XROWS, W)))
    for p in range(ND + 2):
        edge = first_i if p == 0 else last_i if p == ND + 1 else False
        for side, outside in ((0, first_j), (1, last_j)):
            x = jnp.where(outside | edge, jnp.zeros((CI, W), BF), rh[side, p])
            at = side * 48
            xh[p, at:at + CI] = shift_right(x)
            xh[p, at + CI:at + 2 * CI] = x
            xh[p, at + 2 * CI:at + 3 * CI] = shift_left(x)
    bm[0] += dot(tm[:, 0:KM], xa[0])
    bm[ND - 1] += dot(tm[:, 2 * KM:3 * KM], xa[ND + 1])

    def forward(q):
        total = None
        for k in range(2):
            d = 2 * q + k
            rim = dot(th[...], xh[pl.ds(d, 3)].reshape(3 * 128, W))
            own = bm[d]
            before = jnp.concatenate([own[:CO] + rim[:CO], own[CO:ROWS - CO], own[ROWS - CO:] + rim[CO:]], axis=0)
            before = before + bias_rows
            t = jnp.tanh(0.5 * before)
            act = jnp.maximum(before, 0.3 * before) - 0.7 * jnp.log(0.5 + 0.5 * jnp.abs(t))
            slope = (0.08125 + 0.04375 * t).reshape(4, 2, CO, W)
            ga[d, ROWS:2 * ROWS] = (um[q].reshape(4, 1, CO, W) * slope).reshape(ROWS, W).astype(BF)
            part = act.reshape(4, 2, CO, W).sum(axis=1).reshape(128, W)
            total = part if total is None else total + part
        cells[q] = total

    acc[...] = jnp.zeros_like(acc)

    def stage(s, carry):
        forward(2 * s)
        forward(2 * s + 1)
        ds = [4 * s + k for k in range(4)]
        right = jnp.concatenate([ga[d, ROWS:2 * ROWS] for d in ds], axis=1)
        acc[0:3 * KM] += dot_nt(jnp.concatenate([xa[pl.ds(d, 3)].reshape(3 * KM, W) for d in ds], axis=1), right)
        acc[3 * KM:] += dot_nt(jnp.concatenate([xh[pl.ds(d, 3)].reshape(3 * 128, W) for d in ds], axis=1), right)
        return carry

    lax.fori_loop(0, ND // 4, stage, 0)

    def run(count, make, act):
        def step(k, carry):
            getattr(make(k), act)()
            return carry
        lax.fori_loop(1, count, step, 0)

    def pool_copy(k):
        t, target = high_target(k)
        return remote(ps.at[t], rpool.at[j], s_p.at[k], r_p.at[k], target)

    sub, lane_at = iota((1, NH, W), 1), iota((1, NH, W), 2) // CO
    half_at = iota((48, W), 1) // CO
    lane_block = iota((48, 128), 1) // CO

    def fold(x):
        x = x[:, :128] + x[:, 128:]
        x = x + pltpu.roll(x, 64, 1)
        return x + pltpu.roll(x, 32, 1)

    comp[...] = jnp.zeros_like(comp)
    for a in range(3):
        own = acc[a * KM:(a + 1) * KM].reshape(48, NH, W)
        side = 3 * KM + a * 128
        for b in range(3):
            t = a * 3 + b
            diag = jnp.sum(jnp.where(sub == lane_at + (b - 1), own, 0.0), axis=1)
            if b == 0:
                diag = diag + jnp.where(half_at == 0, acc[side:side + 48], 0.0)
            if b == 2:
                diag = diag + jnp.where(half_at == NH - 1, acc[side + 48:side + 96], 0.0)
            diag = fold(diag)
            if t < 8:
                at = (t % 2) * 48
                comp[at:at + 48] += jnp.where(lane_block == t // 2, diag, 0.0)
            else:
                comp[96:128] += jnp.where(lane_block[:32] == 0, diag[:32], 0.0)
                comp[96:112] += jnp.where(lane_block[:16] == 1, diag[32:48], 0.0)
    comp[96:104] += jnp.where(lane_block[:8] == 2, fold(acc[3 * KM + 128 + ONES:3 * KM + 128 + ONES + 8]), 0.0)

    def scatter_copy(k):
        t, target = near_target(k)
        return remote(comp.at[pl.ds(pl.multiple_of(t * PIECE, PIECE), PIECE)], rs.at[near], s_a.at[k], r_a.at[k], target)

    def all_copy(k):
        return remote(piece, rs2.at[far], s_b.at[k], r_b.at[k], far_target(k)[1])

    own_piece = pl.ds(pl.multiple_of(near * PIECE, PIECE), PIECE)

    def gather_copy(k):
        here = full.at[own_piece]
        return remote(here, here, s_c.at[k], r_c.at[k], near_target(k)[1])

    run(NEAR, scatter_copy, "start")
    rs[near] = comp[own_piece]

    for q in range(PAIRS):
        total = cells[q]
        high = total.astype(BF)
        low = (total - high.astype(F32)).astype(BF)
        mean = dot(jnp.concatenate([high, low], axis=1), gather).astype(BF)
        ps[q] = dot(to_o_major, mean).astype(BF).reshape(CO, 4, 128)
    run(nh, pool_copy, "start")
    rpool[j] = ps[j]

    for d in range(ND):
        g = ga[d, ROWS:2 * ROWS]
        ga[d, 0:ROWS] = shift_left(g)
        ga[d, 2 * ROWS:3 * ROWS] = shift_right(g)

    def back(d):
        lo, hi = max(d - 1, 0), min(d + 2, ND)
        k0 = (lo - d + 1) * 3 * ROWS
        n = hi - lo
        return dot(tb[:, k0:k0 + n * 3 * ROWS], ga[lo:hi].reshape(n * 3 * ROWS, W))

    def keep(d, out):
        ph[0, d + 1] = out[XROWS:XROWS + CI].astype(BF)
        ph[1, d + 1] = out[XROWS + CI:].astype(BF)

    for side, d in ((0, -1), (1, ND)):
        out = back(d)
        pd[side] = out[:XROWS].astype(BF)
        keep(d, out)
    grad_copies = [
        remote(pd.at[0], rpd.at[1], s_g.at[0], r_g.at[0], (dn_i, j)),
        remote(pd.at[1], rpd.at[0], s_g.at[1], r_g.at[1], (up_i, j)),
        remote(ph.at[0, 0], rpc.at[1, 1], s_g.at[2], r_g.at[2], (dn_i, dn_j)),
        remote(ph.at[1, 0], rpc.at[1, 0], s_g.at[3], r_g.at[3], (dn_i, up_j)),
        remote(ph.at[0, ND + 1], rpc.at[0, 1], s_g.at[4], r_g.at[4], (up_i, dn_j)),
        remote(ph.at[1, ND + 1], rpc.at[0, 0], s_g.at[5], r_g.at[5], (up_i, up_j)),
    ]
    for copy in grad_copies:
        copy.start()

    def send_rows(n, d, count):
        for side, t in ((0, dn_j), (1, up_j)):
            at = 6 + 2 * n + side
            copy = remote(ph.at[side, pl.ds(d + 1, count)], rp.at[1 - side, pl.ds(d, count)],
                          s_g.at[at], r_g.at[at], (i, t))
            copy.start()
            grad_copies.append(copy)

    for d in (0, ND - 1):
        out = back(d)
        om[d] = out[:XROWS]
        keep(d, out)

    run(NEAR, scatter_copy, "wait_recv")
    total = rs[0]
    for k in range(1, NEAR):
        total = total + rs[k]
    piece[...] = total
    rs2[far] = total
    run(FAR, all_copy, "start")

    def inner(d0, count):
        def step(n, carry):
            for k in range(2):
                d = d0 + 2 * n + k
                out = dot(tb[...], ga[pl.ds(d - 1, 3)].reshape(9 * ROWS, W))
                om[d] = out[:XROWS]
                ph[0, d + 1] = out[XROWS:XROWS + CI].astype(BF)
                ph[1, d + 1] = out[XROWS + CI:].astype(BF)
            return carry
        lax.fori_loop(0, count // 2, step, 0)

    inner(1, 4)
    send_rows(0, 0, 5)
    inner(5, 4)
    send_rows(1, 5, 4)
    inner(9, 6)
    send_rows(2, 9, 7)

    run(FAR, all_copy, "wait_recv")
    total = rs2[0]
    for k in range(1, FAR):
        total = total + rs2[k]
    full[own_piece] = total
    run(NEAR, gather_copy, "start")

    run(nh, pool_copy, "wait_recv")
    for o in range(CO):
        pooled[o, 0] = rpool[:, o].reshape(4 * nh, 128)

    for copy in grad_copies:
        copy.wait_recv()
    row, col = iota((XROWS, 2 * CI), 0), iota((XROWS, 2 * CI), 1)
    place = one_hot(row == (col % CI) * NH + (col // CI) * (NH - 1))
    zero_rows = jnp.zeros((CI, W), BF)

    def edges(low, high, none):
        return dot(place, jnp.concatenate([jnp.where(first_j | none, zero_rows, low),
                                           jnp.where(last_j | none, zero_rows, high)], axis=0))

    for d in range(ND):
        out = om[d] + edges(rp[0, d], rp[1, d], False)
        if d in (0, ND - 1):
            side = 0 if d == 0 else 1
            none = first_i if d == 0 else last_i
            out = out + edges(rpc[side, 0], rpc[side, 1], none)
            out = out + jnp.where(none, zero_slab, rpd[side]).astype(F32)
        gvol[:, d] = out.astype(BF).reshape(CI, NH, W)

    run(NEAR, gather_copy, "wait_recv")
    norm = 1.0 / math.sqrt(float(ND * NH * W * nd * nh))
    final = full[...] * norm
    turned = final.T
    for t in range(8):
        gker[t // 3, t % 3] = turned[(t // 2) * CO:(t // 2 + 1) * CO, (t % 2) * 48:(t % 2 + 1) * 48]
    gker[2, 2, :, 0:32] = turned[0:CO, 96:128]
    gker[2, 2, :, 32:48] = turned[CO:2 * CO, 96:112]
    gbias[...] = final[96:97, 2 * CO:3 * CO]

    for copy in vol_copies + grad_copies:
        copy.wait_send()
    run(nh, pool_copy, "wait_send")
    run(NEAR, scatter_copy, "wait_send")
    run(FAR, all_copy, "wait_send")
    run(NEAR, gather_copy, "wait_send")


def hand_over(*refs):
    n = len(refs) // 2
    for k in range(n):
        refs[n + k][...] = refs[k][...]


def shards(nd, nh, volume, kernel, conv_bias, cotangent):
    vmem = pl.BlockSpec(memory_space=pltpu.VMEM)
    anywhere = pl.BlockSpec(memory_space=pl.ANY)
    dma = pltpu.SemaphoreType.DMA
    out_shape = (
        jax.ShapeDtypeStruct((CO, 1, 4 * nh, 128), BF),
        jax.ShapeDtypeStruct((CI, ND, NH, W), BF),
        jax.ShapeDtypeStruct((3, 3, CO, 3 * CI), F32),
        jax.ShapeDtypeStruct((1, CO), F32),
    )
    results = pl.pallas_call(
        functools.partial(kernel_body, nd, nh),
        out_shape=out_shape,
        in_specs=[anywhere, vmem, vmem, anywhere],
        out_specs=(vmem,) * 4,
        scratch_shapes=[
            pltpu.VMEM((CI, ND, NH, W), BF),
            pltpu.VMEM((CO, PAIRS, 4, 128), BF),
            pltpu.VMEM((ND + 2, KM, W), BF),
            pltpu.VMEM((ND + 2, 128, W), BF),
            pltpu.VMEM((ND, 3 * ROWS, W), BF),
            pltpu.VMEM((ROWS, 3 * KM), BF),
            pltpu.VMEM((2 * CO, 3 * 128), BF),
            pltpu.VMEM((XROWS + 2 * CI, 9 * ROWS), BF),
            pltpu.VMEM((3 * KM + 3 * 128, ROWS), F32),
            pltpu.VMEM((ND, ROWS, W), F32),
            pltpu.VMEM((ND, XROWS, W), F32),
            pltpu.VMEM((PAIRS, 128, W), F32),
            pltpu.VMEM((PAIRS, 128, W), F32),
            pltpu.VMEM((2, ND, CI, W), BF),
            pltpu.VMEM((2, ND + 2, CI, W), BF),
            pltpu.VMEM((2, CI, NH, W), BF),
            pltpu.VMEM((PAIRS, CO, 4, 128), BF),
            pltpu.VMEM((PAIRS, CO, 4, 128), BF),
            pltpu.VMEM((2, ND + 2, CI, W), BF),
            pltpu.VMEM((2, ND, CI, W), BF),
            pltpu.VMEM((2, 2, CI, W), BF),
            pltpu.VMEM((2, XROWS, W), BF),
            pltpu.VMEM((2, XROWS, W), BF),
            pltpu.VMEM((128, 128), F32),
            pltpu.VMEM((NEAR, PIECE, 128), F32),
            pltpu.VMEM((FAR, PIECE, 128), F32),
            pltpu.VMEM((PIECE, 128), F32),
            pltpu.VMEM((128, 128), F32),
            dma((2,)),
            dma((8,)), dma((8,)),
            dma((nh,)), dma((nh,)),
            dma((12,)), dma((12,)),
            dma((NEAR,)), dma((NEAR,)),
            dma((FAR,)), dma((FAR,)),
            dma((NEAR,)), dma((NEAR,)),
        ],
        compiler_params=pltpu.CompilerParams(
            collective_id=0, has_side_effects=True, vmem_limit_bytes=58 * 2**20),
        cost_estimate=pl.CostEstimate(flops=10 * 10**9, bytes_accessed=3 * 2**20, transcendentals=2 * 2**20),
        name="conv_step",
    )(volume, kernel.reshape(3, 3 * CO, 3 * CI), conv_bias.reshape(1, CO), cotangent)
    pooled, gvol, gker, gbias = pl.pallas_call(
        hand_over,
        out_shape=out_shape,
        in_specs=[vmem] * 4,
        out_specs=(vmem,) * 4,
        name="hand_over",
    )(*results)
    return pooled, gvol, gker, gbias.reshape(CO)


def solution(mesh):
    nd, nh = mesh.shape["depth"], mesh.shape["height"]
    in_specs = (P(None, "depth", "height", None), P(), P(), P(None, "depth", "height", None))
    out_specs = (
        P(None, ("depth", "height"), None, None),
        P(None, "depth", "height", None),
        P(),
        P(),
    )
    return jax.shard_map(
        functools.partial(shards, nd, nh), mesh=mesh, in_specs=in_specs, out_specs=out_specs, check_vma=False)
```

```python
import functools
import math

import jax
import jax.numpy as jnp
from jax import lax
from jax.experimental import pallas as pl
from jax.experimental.pallas import tpu as pltpu
from jax.sharding import PartitionSpec as P

BF = jnp.bfloat16
F32 = jnp.float32
MESH = pl.DeviceIdType.MESH

CI, CO, ND, NH, W = 16, 32, 16, 8, 256
ROWS = CO * NH
XROWS = CI * NH
KM = 3 * XROWS
ONES = 96
PAIRS = ND // 2
RING = 4
NEAR = 8
FAR = RING * RING
PIECE = 128 // NEAR


def dot(a, b):
    return jnp.dot(a, b, preferred_element_type=F32)


def dot_nt(a, b):
    return lax.dot_general(a, b, (((1,), (1,)), ((), ())), preferred_element_type=F32)


def iota(shape, dim):
    return lax.broadcasted_iota(jnp.int32, shape, dim)


def one_hot(cond, value=1.0):
    return jnp.where(cond, value, 0.0).astype(BF)


def shift_right(x):
    rolled = pltpu.roll(x, 1, 1)
    return jnp.where(iota(x.shape, 1) == 0, jnp.zeros_like(x), rolled)


def shift_left(x):
    rolled = pltpu.roll(x, x.shape[1] - 1, 1)
    return jnp.where(iota(x.shape, 1) == x.shape[1] - 1, jnp.zeros_like(x), rolled)


def kernel_body(nd, nh, vol_in, ker, bias, cot_in, pooled, gvol, gker, gbias,
                vol, cot, xa, xh, ga, tm, th, tb, acc, bm, om, um, cells, hs, rh, rd, ps, rpool, ph, rp, rpc, pd, rpd, comp, rs, rs2, piece,
                full, s_in, s_v, r_v, s_p, r_p, s_g, r_g, s_a, r_a, s_b, r_b, s_c, r_c, known):
    i = lax.axis_index("depth")
    j = lax.axis_index("height")
    up_i, dn_i = lax.rem(i + 1, nd), lax.rem(i + nd - 1, nd)
    up_j, dn_j = lax.rem(j + 1, nh), lax.rem(j + nh - 1, nh)
    first_i, last_i = i == 0, i == nd - 1
    first_j, last_j = j == 0, j == nh - 1
    near = lax.rem(j, 2) * 4 + lax.rem(i, 4)
    far = (i // 4) * RING + j // 2

    def near_target(k):
        t = lax.rem(near + k, NEAR)
        return t, ((i // 4) * 4 + lax.rem(t, 4), (j // 2) * 2 + t // 4)

    def far_target(k):
        t = lax.rem(far + k, FAR)
        return t, ((t // RING) * 4 + lax.rem(i, 4), lax.rem(t, RING) * 2 + lax.rem(j, 2))

    def high_target(k):
        t = lax.rem(j + k, nh)
        return t, (i, t)

    vol_load = pltpu.make_async_copy(vol_in, vol, s_in.at[0])
    cot_load = pltpu.make_async_copy(cot_in, cot, s_in.at[1])
    vol_load.start()
    cot_load.start()
    barrier = pltpu.get_barrier_semaphore()

    def greet(sem, targets):
        for target in targets:
            pl.semaphore_signal(sem, inc=1, device_id=target, device_id_type=MESH)

    def around(n):
        at_i = (lax.rem(i + nd - n, nd), i, lax.rem(i + n, nd))
        at_j = (lax.rem(j + nh - n, nh), j, lax.rem(j + n, nh))
        return [(at_i[a], at_j[b]) for a in range(3) for b in range(3) if (a, b) != (1, 1)]

    greet(barrier, around(1))

    row, col = iota((2 * CI, XROWS), 0), iota((2 * CI, XROWS), 1)
    edge_rows = one_hot(col == (row % CI) * NH + (row // CI) * (NH - 1))
    vol_load.wait()
    for d in range(ND):
        edge = dot(edge_rows, vol[:, d].reshape(XROWS, W)).astype(BF)
        hs[0, d] = edge[:CI]
        hs[1, d] = edge[CI:]

    pl.semaphore_wait(barrier, 8)
    greet(known.at[0], around(1))

    def remote(src, dst, send, recv, target):
        return pltpu.make_async_remote_copy(
            src_ref=src, dst_ref=dst, send_sem=send, recv_sem=recv, device_id=target, device_id_type=MESH)

    vol_copies = [
        remote(vol.at[:, 0], rd.at[1], s_v.at[0], r_v.at[0], (dn_i, j)),
        remote(vol.at[:, ND - 1], rd.at[0], s_v.at[1], r_v.at[1], (up_i, j)),
        remote(hs.at[0, 0], rh.at[1, ND + 1], s_v.at[2], r_v.at[2], (dn_i, dn_j)),
        remote(hs.at[0, ND - 1], rh.at[1, 0], s_v.at[3], r_v.at[3], (up_i, dn_j)),
        remote(hs.at[1, 0], rh.at[0, ND + 1], s_v.at[4], r_v.at[4], (dn_i, up_j)),
        remote(hs.at[1, ND - 1], rh.at[0, 0], s_v.at[5], r_v.at[5], (up_i, up_j)),
        remote(hs.at[0], rh.at[1, pl.ds(1, ND)], s_v.at[6], r_v.at[6], (i, dn_j)),
        remote(hs.at[1], rh.at[0, pl.ds(1, ND)], s_v.at[7], r_v.at[7], (i, up_j)),
    ]
    for copy in vol_copies:
        copy.start()

    def put_slab(p, x):
        xa[p, 0:XROWS] = shift_right(x)
        xa[p, XROWS:2 * XROWS] = x
        xa[p, 2 * XROWS:3 * XROWS] = shift_left(x)

    for d in range(ND):
        put_slab(d + 1, vol[:, d].reshape(XROWS, W))

    row, col = iota((3 * CI, 640), 0), iota((3 * CI, 640), 1)
    expand = one_hot(((col < 384) & (row == col // NH))
                     | ((col >= 384) & (col < 512) & (row == col - 384))
                     | ((col >= 512) & (row + 3 * CI == col - 512)))
    lane_h = iota((CO, 384), 1) % NH
    for a in range(3):
        taps = dot(ker[a], expand)
        for h in range(NH):
            band = jnp.zeros((CO, 384), F32)
            for b in range(3):
                if 0 <= h + b - 1 < NH:
                    band = jnp.where(lane_h == h + b - 1, taps[b * CO:(b + 1) * CO, :384], band)
            tm[h * CO:(h + 1) * CO, a * KM:(a + 1) * KM] = band.astype(BF)
        th[0:CO, a * 128:(a + 1) * 128] = taps[0:CO, 384:512].astype(BF)
        th[CO:2 * CO, a * 128:(a + 1) * 128] = taps[2 * CO:3 * CO, 512:640].astype(BF)

    pl.semaphore_wait(known.at[0], 8)
    greet(known.at[1], around(2))

    def own_part(d):
        lo, hi = max(d, 1), min(d + 3, ND + 1)
        k0 = (lo - d) * KM
        bm[d] = dot(tm[:, k0:k0 + (hi - lo) * KM], xa[lo:hi].reshape((hi - lo) * KM, W))

    def own_parts(n, carry):
        for k in range(7):
            d = 1 + 7 * n + k
            bm[d] = dot(tm[...], xa[pl.ds(d, 3)].reshape(3 * KM, W))
        return carry

    lax.fori_loop(0, 2, own_parts, 0)
    own_part(0)
    own_part(ND - 1)

    row, col = iota((128, 128), 0), iota((128, 128), 1)
    to_h_major = one_hot(col == (row % CO) * 4 + row // CO)
    to_o_major = one_hot(col == (row % 4) * CO + row // 4)
    spread = one_hot(iota((128, W), 0) == iota((128, W), 1) // 2)
    gather = one_hot((iota((2 * W, 128), 0) % W) // 2 == iota((2 * W, 128), 1), 0.125)
    cot_load.wait()
    for q in range(PAIRS):
        ct = cot[:, q].reshape(128, 128)
        um[q] = dot(dot(to_h_major, ct).astype(BF), spread)
    eye = iota((CO, CO), 0) == iota((CO, CO), 1)
    bias_col = jnp.sum(jnp.where(eye, jnp.broadcast_to(bias[...], (CO, CO)), 0.0), axis=1, keepdims=True)
    bias_rows = jnp.concatenate([bias_col] * NH, axis=0)

    ones_rows = one_hot(iota((128 - ONES, W), 0) == 0)
    for p in range(ND + 2):
        xh[p, ONES:128] = ones_rows

    for a in range(3):
        flipped = tm[:, a * KM:(a + 1) * KM].T
        side = jnp.concatenate([th[0:CO, a * 128:(a + 1) * 128], jnp.zeros((ROWS - 2 * CO, 128), BF),
                                th[CO:2 * CO, a * 128:(a + 1) * 128]], axis=0).T
        for e in range(3):
            at = (2 - a) * 3 * ROWS + e * ROWS
            tb[0:XROWS, at:at + ROWS] = flipped[e * XROWS:(e + 1) * XROWS]
            tb[XROWS:XROWS + CI, at:at + ROWS] = side[e * CI:(e + 1) * CI]
            tb[XROWS + CI:XROWS + 2 * CI, at:at + ROWS] = side[48 + e * CI:48 + (e + 1) * CI]

    pl.semaphore_wait(known.at[1], 8)
    far_apart = [(lax.rem(i + 4, nd), j), (lax.rem(i + nd - 4, nd), j)]
    greet(known.at[2], far_apart)

    for copy in vol_copies:
        copy.wait_recv()
    zero_slab = jnp.zeros((XROWS, W), BF)
    put_slab(0, jnp.where(first_i, zero_slab, rd[0].reshape(XROWS, W)))
    put_slab(ND + 1, jnp.where(last_i, zero_slab, rd[1].reshape(XROWS, W)))
    for p in range(ND + 2):
        edge = first_i if p == 0 else last_i if p == ND + 1 else False
        for side, outside in ((0, first_j), (1, last_j)):
            x = jnp.where(outside | edge, jnp.zeros((CI, W), BF), rh[side, p])
            at = side * 48
            xh[p, at:at + CI] = shift_right(x)
            xh[p, at + CI:at + 2 * CI] = x
            xh[p, at + 2 * CI:at + 3 * CI] = shift_left(x)
    bm[0] += dot(tm[:, 0:KM], xa[0])
    bm[ND - 1] += dot(tm[:, 2 * KM:3 * KM], xa[ND + 1])

    def forward(q):
        total = None
        for k in range(2):
            d = 2 * q + k
            rim = dot(th[...], xh[pl.ds(d, 3)].reshape(3 * 128, W))
            own = bm[d]
            before = jnp.concatenate([own[:CO] + rim[:CO], own[CO:ROWS - CO], own[ROWS - CO:] + rim[CO:]], axis=0)
            before = before + bias_rows
            t = jnp.tanh(0.5 * before)
            act = jnp.maximum(before, 0.3 * before) - 0.7 * jnp.log(0.5 + 0.5 * jnp.abs(t))
            slope = (0.08125 + 0.04375 * t).reshape(4, 2, CO, W)
            ga[d, ROWS:2 * ROWS] = (um[q].reshape(4, 1, CO, W) * slope).reshape(ROWS, W).astype(BF)
            part = act.reshape(4, 2, CO, W).sum(axis=1).reshape(128, W)
            total = part if total is None else total + part
        cells[q] = total

    acc[...] = jnp.zeros_like(acc)

    def stage(s, carry):
        forward(2 * s)
        forward(2 * s + 1)
        ds = [4 * s + k for k in range(4)]
        right = jnp.concatenate([ga[d, ROWS:2 * ROWS] for d in ds], axis=1)
        acc[0:3 * KM] += dot_nt(jnp.concatenate([xa[pl.ds(d, 3)].reshape(3 * KM, W) for d in ds], axis=1), right)
        acc[3 * KM:] += dot_nt(jnp.concatenate([xh[pl.ds(d, 3)].reshape(3 * 128, W) for d in ds], axis=1), right)
        return carry

    lax.fori_loop(0, ND // 4, stage, 0)

    def run(count, make, act):
        def step(k, carry):
            getattr(make(k), act)()
            return carry
        lax.fori_loop(1, count, step, 0)

    def pool_copy(k):
        t, target = high_target(k)
        return remote(ps.at[t], rpool.at[j], s_p.at[k], r_p.at[k], target)

    sub, lane_at = iota((1, NH, W), 1), iota((1, NH, W), 2) // CO
    half_at = iota((48, W), 1) // CO
    lane_block = iota((48, 128), 1) // CO

    def fold(x):
        x = x[:, :128] + x[:, 128:]
        x = x + pltpu.roll(x, 64, 1)
        return x + pltpu.roll(x, 32, 1)

    comp[...] = jnp.zeros_like(comp)
    for a in range(3):
        own = acc[a * KM:(a + 1) * KM].reshape(48, NH, W)
        side = 3 * KM + a * 128
        for b in range(3):
            t = a * 3 + b
            diag = jnp.sum(jnp.where(sub == lane_at + (b - 1), own, 0.0), axis=1)
            if b == 0:
                diag = diag + jnp.where(half_at == 0, acc[side:side + 48], 0.0)
            if b == 2:
                diag = diag + jnp.where(half_at == NH - 1, acc[side + 48:side + 96], 0.0)
            diag = fold(diag)
            if t < 8:
                at = (t % 2) * 48
                comp[at:at + 48] += jnp.where(lane_block == t // 2, diag, 0.0)
            else:
                comp[96:128] += jnp.where(lane_block[:32] == 0, diag[:32], 0.0)
                comp[96:112] += jnp.where(lane_block[:16] == 1, diag[32:48], 0.0)
    comp[96:104] += jnp.where(lane_block[:8] == 2, fold(acc[3 * KM + 128 + ONES:3 * KM + 128 + ONES + 8]), 0.0)

    def scatter_copy(k):
        t, target = near_target(k)
        return remote(comp.at[pl.ds(pl.multiple_of(t * PIECE, PIECE), PIECE)], rs.at[near], s_a.at[k], r_a.at[k], target)

    def all_copy(k):
        return remote(piece, rs2.at[far], s_b.at[k], r_b.at[k], far_target(k)[1])

    own_piece = pl.ds(pl.multiple_of(near * PIECE, PIECE), PIECE)

    def gather_copy(k):
        here = full.at[own_piece]
        return remote(here, here, s_c.at[k], r_c.at[k], near_target(k)[1])

    pl.semaphore_wait(known.at[2], 2)
    run(NEAR, scatter_copy, "start")
    rs[near] = comp[own_piece]

    for q in range(PAIRS):
        total = cells[q]
        high = total.astype(BF)
        low = (total - high.astype(F32)).astype(BF)
        mean = dot(jnp.concatenate([high, low], axis=1), gather).astype(BF)
        ps[q] = dot(to_o_major, mean).astype(BF).reshape(CO, 4, 128)
    run(nh, pool_copy, "start")
    rpool[j] = ps[j]

    for d in range(ND):
        g = ga[d, ROWS:2 * ROWS]
        ga[d, 0:ROWS] = shift_left(g)
        ga[d, 2 * ROWS:3 * ROWS] = shift_right(g)

    def back(d):
        lo, hi = max(d - 1, 0), min(d + 2, ND)
        k0 = (lo - d + 1) * 3 * ROWS
        n = hi - lo
        return dot(tb[:, k0:k0 + n * 3 * ROWS], ga[lo:hi].reshape(n * 3 * ROWS, W))

    def keep(d, out):
        ph[0, d + 1] = out[XROWS:XROWS + CI].astype(BF)
        ph[1, d + 1] = out[XROWS + CI:].astype(BF)

    for side, d in ((0, -1), (1, ND)):
        out = back(d)
        pd[side] = out[:XROWS].astype(BF)
        keep(d, out)
    grad_copies = [
        remote(pd.at[0], rpd.at[1], s_g.at[0], r_g.at[0], (dn_i, j)),
        remote(pd.at[1], rpd.at[0], s_g.at[1], r_g.at[1], (up_i, j)),
        remote(ph.at[0, 0], rpc.at[1, 1], s_g.at[2], r_g.at[2], (dn_i, dn_j)),
        remote(ph.at[1, 0], rpc.at[1, 0], s_g.at[3], r_g.at[3], (dn_i, up_j)),
        remote(ph.at[0, ND + 1], rpc.at[0, 1], s_g.at[4], r_g.at[4], (up_i, dn_j)),
        remote(ph.at[1, ND + 1], rpc.at[0, 0], s_g.at[5], r_g.at[5], (up_i, up_j)),
    ]
    for copy in grad_copies:
        copy.start()

    def send_rows(n, d, count):
        for side, t in ((0, dn_j), (1, up_j)):
            at = 6 + 2 * n + side
            copy = remote(ph.at[side, pl.ds(d + 1, count)], rp.at[1 - side, pl.ds(d, count)],
                          s_g.at[at], r_g.at[at], (i, t))
            copy.start()
            grad_copies.append(copy)

    for d in (0, ND - 1):
        out = back(d)
        om[d] = out[:XROWS]
        keep(d, out)

    run(NEAR, scatter_copy, "wait_recv")
    total = rs[0]
    for k in range(1, NEAR):
        total = total + rs[k]
    piece[...] = total
    rs2[far] = total
    run(FAR, all_copy, "start")

    def inner(d0, count):
        def step(n, carry):
            for k in range(2):
                d = d0 + 2 * n + k
                out = dot(tb[...], ga[pl.ds(d - 1, 3)].reshape(9 * ROWS, W))
                om[d] = out[:XROWS]
                ph[0, d + 1] = out[XROWS:XROWS + CI].astype(BF)
                ph[1, d + 1] = out[XROWS + CI:].astype(BF)
            return carry
        lax.fori_loop(0, count // 2, step, 0)

    inner(1, 4)
    send_rows(0, 0, 5)
    inner(5, 4)
    send_rows(1, 5, 4)
    inner(9, 6)
    send_rows(2, 9, 7)

    run(FAR, all_copy, "wait_recv")
    total = rs2[0]
    for k in range(1, FAR):
        total = total + rs2[k]
    full[own_piece] = total
    run(NEAR, gather_copy, "start")

    run(nh, pool_copy, "wait_recv")
    for o in range(CO):
        pooled[o, 0] = rpool[:, o].reshape(4 * nh, 128)

    for copy in grad_copies:
        copy.wait_recv()
    row, col = iota((XROWS, 2 * CI), 0), iota((XROWS, 2 * CI), 1)
    place = one_hot(row == (col % CI) * NH + (col // CI) * (NH - 1))
    zero_rows = jnp.zeros((CI, W), BF)

    def edges(low, high, none):
        return dot(place, jnp.concatenate([jnp.where(first_j | none, zero_rows, low),
                                           jnp.where(last_j | none, zero_rows, high)], axis=0))

    for d in range(ND):
        out = om[d] + edges(rp[0, d], rp[1, d], False)
        if d in (0, ND - 1):
            side = 0 if d == 0 else 1
            none = first_i if d == 0 else last_i
            out = out + edges(rpc[side, 0], rpc[side, 1], none)
            out = out + jnp.where(none, zero_slab, rpd[side]).astype(F32)
        gvol[:, d] = out.astype(BF).reshape(CI, NH, W)

    run(NEAR, gather_copy, "wait_recv")
    norm = 1.0 / math.sqrt(float(ND * NH * W * nd * nh))
    final = full[...] * norm
    turned = final.T
    for t in range(8):
        gker[t // 3, t % 3] = turned[(t // 2) * CO:(t // 2 + 1) * CO, (t % 2) * 48:(t % 2 + 1) * 48]
    gker[2, 2, :, 0:32] = turned[0:CO, 96:128]
    gker[2, 2, :, 32:48] = turned[CO:2 * CO, 96:112]
    gbias[...] = final[96:97, 2 * CO:3 * CO]

    for copy in vol_copies + grad_copies:
        copy.wait_send()
    run(nh, pool_copy, "wait_send")
    run(NEAR, scatter_copy, "wait_send")
    run(FAR, all_copy, "wait_send")
    run(NEAR, gather_copy, "wait_send")


def hand_over(*refs):
    n = len(refs) // 2
    for k in range(n):
        refs[n + k][...] = refs[k][...]


def shards(nd, nh, volume, kernel, conv_bias, cotangent):
    vmem = pl.BlockSpec(memory_space=pltpu.VMEM)
    anywhere = pl.BlockSpec(memory_space=pl.ANY)
    dma = pltpu.SemaphoreType.DMA
    out_shape = (
        jax.ShapeDtypeStruct((CO, 1, 4 * nh, 128), BF),
        jax.ShapeDtypeStruct((CI, ND, NH, W), BF),
        jax.ShapeDtypeStruct((3, 3, CO, 3 * CI), F32),
        jax.ShapeDtypeStruct((1, CO), F32),
    )
    results = pl.pallas_call(
        functools.partial(kernel_body, nd, nh),
        out_shape=out_shape,
        in_specs=[anywhere, vmem, vmem, anywhere],
        out_specs=(vmem,) * 4,
        scratch_shapes=[
            pltpu.VMEM((CI, ND, NH, W), BF),
            pltpu.VMEM((CO, PAIRS, 4, 128), BF),
            pltpu.VMEM((ND + 2, KM, W), BF),
            pltpu.VMEM((ND + 2, 128, W), BF),
            pltpu.VMEM((ND, 3 * ROWS, W), BF),
            pltpu.VMEM((ROWS, 3 * KM), BF),
            pltpu.VMEM((2 * CO, 3 * 128), BF),
            pltpu.VMEM((XROWS + 2 * CI, 9 * ROWS), BF),
            pltpu.VMEM((3 * KM + 3 * 128, ROWS), F32),
            pltpu.VMEM((ND, ROWS, W), F32),
            pltpu.VMEM((ND, XROWS, W), F32),
            pltpu.VMEM((PAIRS, 128, W), F32),
            pltpu.VMEM((PAIRS, 128, W), F32),
            pltpu.VMEM((2, ND, CI, W), BF),
            pltpu.VMEM((2, ND + 2, CI, W), BF),
            pltpu.VMEM((2, CI, NH, W), BF),
            pltpu.VMEM((PAIRS, CO, 4, 128), BF),
            pltpu.VMEM((PAIRS, CO, 4, 128), BF),
            pltpu.VMEM((2, ND + 2, CI, W), BF),
            pltpu.VMEM((2, ND, CI, W), BF),
            pltpu.VMEM((2, 2, CI, W), BF),
            pltpu.VMEM((2, XROWS, W), BF),
            pltpu.VMEM((2, XROWS, W), BF),
            pltpu.VMEM((128, 128), F32),
            pltpu.VMEM((NEAR, PIECE, 128), F32),
            pltpu.VMEM((FAR, PIECE, 128), F32),
            pltpu.VMEM((PIECE, 128), F32),
            pltpu.VMEM((128, 128), F32),
            dma((2,)),
            dma((8,)), dma((8,)),
            dma((nh,)), dma((nh,)),
            dma((12,)), dma((12,)),
            dma((NEAR,)), dma((NEAR,)),
            dma((FAR,)), dma((FAR,)),
            dma((NEAR,)), dma((NEAR,)),
            pltpu.SemaphoreType.REGULAR((3,)),
        ],
        compiler_params=pltpu.CompilerParams(
            collective_id=0, has_side_effects=True, vmem_limit_bytes=58 * 2**20),
        cost_estimate=pl.CostEstimate(flops=10 * 10**9, bytes_accessed=3 * 2**20, transcendentals=2 * 2**20),
        name="conv_step",
    )(volume, kernel.reshape(3, 3 * CO, 3 * CI), conv_bias.reshape(1, CO), cotangent)
    pooled, gvol, gker, gbias = pl.pallas_call(
        hand_over,
        out_shape=out_shape,
        in_specs=[vmem] * 4,
        out_specs=(vmem,) * 4,
        name="hand_over",
    )(*results)
    return pooled, gvol, gker, gbias.reshape(CO)


def solution(mesh):
    nd, nh = mesh.shape["depth"], mesh.shape["height"]
    in_specs = (P(None, "depth", "height", None), P(), P(), P(None, "depth", "height", None))
    out_specs = (
        P(None, ("depth", "height"), None, None),
        P(None, "depth", "height", None),
        P(),
        P(),
    )
    return jax.shard_map(
        functools.partial(shards, nd, nh), mesh=mesh, in_specs=in_specs, out_specs=out_specs, check_vma=False)
```

```python
import functools
import math

import jax
import jax.numpy as jnp
from jax import lax
from jax.experimental import pallas as pl
from jax.experimental.pallas import tpu as pltpu
from jax.sharding import PartitionSpec as P

BF = jnp.bfloat16
F32 = jnp.float32
MESH = pl.DeviceIdType.MESH

CI, CO, ND, NH, W = 16, 32, 16, 8, 256
ROWS = CO * NH
XROWS = CI * NH
KM = 3 * XROWS
ONES = 96
PAIRS = ND // 2
RING = 4
NEAR = 8
FAR = RING * RING
PIECE = 128 // NEAR


def dot(a, b):
    return jnp.dot(a, b, preferred_element_type=F32)


def dot_nt(a, b):
    return lax.dot_general(a, b, (((1,), (1,)), ((), ())), preferred_element_type=F32)


def iota(shape, dim):
    return lax.broadcasted_iota(jnp.int32, shape, dim)


def one_hot(cond, value=1.0):
    return jnp.where(cond, value, 0.0).astype(BF)


def shift_right(x):
    rolled = pltpu.roll(x, 1, 1)
    return jnp.where(iota(x.shape, 1) == 0, jnp.zeros_like(x), rolled)


def shift_left(x):
    rolled = pltpu.roll(x, x.shape[1] - 1, 1)
    return jnp.where(iota(x.shape, 1) == x.shape[1] - 1, jnp.zeros_like(x), rolled)


def kernel_body(nd, nh, vol_in, ker, bias, cot_in, pooled_out, gvol_out, gker, gbias,
                vol, cot, xa, xh, ga, tm, th, tb, acc, bm, om, um, cells, hs, rh, rd, ps, rpool, ph, rp, rpc, pd, rpd, comp, rs, rs2, piece,
                full, pooled, gvol, s_in, s_o, s_v, r_v, s_p, r_p, s_g, r_g, s_a, r_a, s_b, r_b, s_c, r_c, known):
    i = lax.axis_index("depth")
    j = lax.axis_index("height")
    up_i, dn_i = lax.rem(i + 1, nd), lax.rem(i + nd - 1, nd)
    up_j, dn_j = lax.rem(j + 1, nh), lax.rem(j + nh - 1, nh)
    first_i, last_i = i == 0, i == nd - 1
    first_j, last_j = j == 0, j == nh - 1
    near = lax.rem(j, 2) * 4 + lax.rem(i, 4)
    far = (i // 4) * RING + j // 2

    def near_target(k):
        t = lax.rem(near + k, NEAR)
        return t, ((i // 4) * 4 + lax.rem(t, 4), (j // 2) * 2 + t // 4)

    def far_target(k):
        t = lax.rem(far + k, FAR)
        return t, ((t // RING) * 4 + lax.rem(i, 4), lax.rem(t, RING) * 2 + lax.rem(j, 2))

    def high_target(k):
        t = lax.rem(j + k, nh)
        return t, (i, t)

    vol_load = pltpu.make_async_copy(vol_in, vol, s_in.at[0])
    cot_load = pltpu.make_async_copy(cot_in, cot, s_in.at[1])
    vol_load.start()
    cot_load.start()
    barrier = pltpu.get_barrier_semaphore()

    def greet(sem, targets):
        for target in targets:
            pl.semaphore_signal(sem, inc=1, device_id=target, device_id_type=MESH)

    def around(n):
        at_i = (lax.rem(i + nd - n, nd), i, lax.rem(i + n, nd))
        at_j = (lax.rem(j + nh - n, nh), j, lax.rem(j + n, nh))
        return [(at_i[a], at_j[b]) for a in range(3) for b in range(3) if (a, b) != (1, 1)]

    greet(barrier, around(1))

    row, col = iota((2 * CI, XROWS), 0), iota((2 * CI, XROWS), 1)
    edge_rows = one_hot(col == (row % CI) * NH + (row // CI) * (NH - 1))
    vol_load.wait()
    for d in range(ND):
        edge = dot(edge_rows, vol[:, d].reshape(XROWS, W)).astype(BF)
        hs[0, d] = edge[:CI]
        hs[1, d] = edge[CI:]

    pl.semaphore_wait(barrier, 8)
    greet(known.at[0], around(1))

    def remote(src, dst, send, recv, target):
        return pltpu.make_async_remote_copy(
            src_ref=src, dst_ref=dst, send_sem=send, recv_sem=recv, device_id=target, device_id_type=MESH)

    vol_copies = [
        remote(vol.at[:, 0], rd.at[1], s_v.at[0], r_v.at[0], (dn_i, j)),
        remote(vol.at[:, ND - 1], rd.at[0], s_v.at[1], r_v.at[1], (up_i, j)),
        remote(hs.at[0, 0], rh.at[1, ND + 1], s_v.at[2], r_v.at[2], (dn_i, dn_j)),
        remote(hs.at[0, ND - 1], rh.at[1, 0], s_v.at[3], r_v.at[3], (up_i, dn_j)),
        remote(hs.at[1, 0], rh.at[0, ND + 1], s_v.at[4], r_v.at[4], (dn_i, up_j)),
        remote(hs.at[1, ND - 1], rh.at[0, 0], s_v.at[5], r_v.at[5], (up_i, up_j)),
        remote(hs.at[0], rh.at[1, pl.ds(1, ND)], s_v.at[6], r_v.at[6], (i, dn_j)),
        remote(hs.at[1], rh.at[0, pl.ds(1, ND)], s_v.at[7], r_v.at[7], (i, up_j)),
    ]
    for copy in vol_copies:
        copy.start()

    def put_slab(p, x):
        xa[p, 0:XROWS] = shift_right(x)
        xa[p, XROWS:2 * XROWS] = x
        xa[p, 2 * XROWS:3 * XROWS] = shift_left(x)

    for d in range(ND):
        put_slab(d + 1, vol[:, d].reshape(XROWS, W))

    row, col = iota((3 * CI, 640), 0), iota((3 * CI, 640), 1)
    expand = one_hot(((col < 384) & (row == col // NH))
                     | ((col >= 384) & (col < 512) & (row == col - 384))
                     | ((col >= 512) & (row + 3 * CI == col - 512)))
    lane_h = iota((CO, 384), 1) % NH
    for a in range(3):
        taps = dot(ker[a], expand)
        for h in range(NH):
            band = jnp.zeros((CO, 384), F32)
            for b in range(3):
                if 0 <= h + b - 1 < NH:
                    band = jnp.where(lane_h == h + b - 1, taps[b * CO:(b + 1) * CO, :384], band)
            tm[h * CO:(h + 1) * CO, a * KM:(a + 1) * KM] = band.astype(BF)
        th[0:CO, a * 128:(a + 1) * 128] = taps[0:CO, 384:512].astype(BF)
        th[CO:2 * CO, a * 128:(a + 1) * 128] = taps[2 * CO:3 * CO, 512:640].astype(BF)

    pl.semaphore_wait(known.at[0], 8)
    greet(known.at[1], around(2))

    def own_part(d):
        lo, hi = max(d, 1), min(d + 3, ND + 1)
        k0 = (lo - d) * KM
        bm[d] = dot(tm[:, k0:k0 + (hi - lo) * KM], xa[lo:hi].reshape((hi - lo) * KM, W))

    def own_parts(n, carry):
        for k in range(7):
            d = 1 + 7 * n + k
            bm[d] = dot(tm[...], xa[pl.ds(d, 3)].reshape(3 * KM, W))
        return carry

    lax.fori_loop(0, 2, own_parts, 0)
    own_part(0)
    own_part(ND - 1)

    row, col = iota((128, 128), 0), iota((128, 128), 1)
    to_h_major = one_hot(col == (row % CO) * 4 + row // CO)
    to_o_major = one_hot(col == (row % 4) * CO + row // 4)
    spread = one_hot(iota((128, W), 0) == iota((128, W), 1) // 2)
    gather = one_hot((iota((2 * W, 128), 0) % W) // 2 == iota((2 * W, 128), 1), 0.125)
    cot_load.wait()
    for q in range(PAIRS):
        ct = cot[:, q].reshape(128, 128)
        um[q] = dot(dot(to_h_major, ct).astype(BF), spread)
    eye = iota((CO, CO), 0) == iota((CO, CO), 1)
    bias_col = jnp.sum(jnp.where(eye, jnp.broadcast_to(bias[...], (CO, CO)), 0.0), axis=1, keepdims=True)
    bias_rows = jnp.concatenate([bias_col] * NH, axis=0)

    ones_rows = one_hot(iota((128 - ONES, W), 0) == 0)
    for p in range(ND + 2):
        xh[p, ONES:128] = ones_rows

    for a in range(3):
        flipped = tm[:, a * KM:(a + 1) * KM].T
        side = jnp.concatenate([th[0:CO, a * 128:(a + 1) * 128], jnp.zeros((ROWS - 2 * CO, 128), BF),
                                th[CO:2 * CO, a * 128:(a + 1) * 128]], axis=0).T
        for e in range(3):
            at = (2 - a) * 3 * ROWS + e * ROWS
            tb[0:XROWS, at:at + ROWS] = flipped[e * XROWS:(e + 1) * XROWS]
            tb[XROWS:XROWS + CI, at:at + ROWS] = side[e * CI:(e + 1) * CI]
            tb[XROWS + CI:XROWS + 2 * CI, at:at + ROWS] = side[48 + e * CI:48 + (e + 1) * CI]

    pl.semaphore_wait(known.at[1], 8)
    far_apart = [(lax.rem(i + 4, nd), j), (lax.rem(i + nd - 4, nd), j)]
    greet(known.at[2], far_apart)

    for copy in vol_copies:
        copy.wait_recv()
    zero_slab = jnp.zeros((XROWS, W), BF)
    put_slab(0, jnp.where(first_i, zero_slab, rd[0].reshape(XROWS, W)))
    put_slab(ND + 1, jnp.where(last_i, zero_slab, rd[1].reshape(XROWS, W)))
    for p in range(ND + 2):
        edge = first_i if p == 0 else last_i if p == ND + 1 else False
        for side, outside in ((0, first_j), (1, last_j)):
            x = jnp.where(outside | edge, jnp.zeros((CI, W), BF), rh[side, p])
            at = side * 48
            xh[p, at:at + CI] = shift_right(x)
            xh[p, at + CI:at + 2 * CI] = x
            xh[p, at + 2 * CI:at + 3 * CI] = shift_left(x)
    bm[0] += dot(tm[:, 0:KM], xa[0])
    bm[ND - 1] += dot(tm[:, 2 * KM:3 * KM], xa[ND + 1])

    def forward(q):
        total = None
        for k in range(2):
            d = 2 * q + k
            rim = dot(th[...], xh[d:d + 3].reshape(3 * 128, W))
            own = bm[d]
            before = jnp.concatenate([own[:CO] + rim[:CO], own[CO:ROWS - CO], own[ROWS - CO:] + rim[CO:]], axis=0)
            before = before + bias_rows
            t = jnp.tanh(0.5 * before)
            act = jnp.maximum(before, 0.3 * before) - 0.7 * jnp.log(0.5 + 0.5 * jnp.abs(t))
            slope = (0.08125 + 0.04375 * t).reshape(4, 2, CO, W)
            ga[d, ROWS:2 * ROWS] = (um[q].reshape(4, 1, CO, W) * slope).reshape(ROWS, W).astype(BF)
            part = act.reshape(4, 2, CO, W).sum(axis=1).reshape(128, W)
            total = part if total is None else total + part
        cells[q] = total

    def taps_grad(s):
        ds = [4 * s + k for k in range(4)]
        right = jnp.concatenate([ga[d, ROWS:2 * ROWS] for d in ds], axis=1)
        own = dot_nt(jnp.concatenate([xa[d:d + 3].reshape(3 * KM, W) for d in ds], axis=1), right)
        rim = dot_nt(jnp.concatenate([xh[d:d + 3].reshape(3 * 128, W) for d in ds], axis=1), right)
        if s == 0:
            acc[0:3 * KM] = own
            acc[3 * KM:] = rim
        else:
            acc[0:3 * KM] += own
            acc[3 * KM:] += rim

    stages = ND // 4
    for s in range(stages + 1):
        if s < stages:
            forward(2 * s)
            forward(2 * s + 1)
        if s > 0:
            taps_grad(s - 1)

    def run(count, make, act):
        def step(k, carry):
            getattr(make(k), act)()
            return carry
        lax.fori_loop(1, count, step, 0)

    def pool_copy(k):
        t, target = high_target(k)
        return remote(ps.at[t], rpool.at[j], s_p.at[k], r_p.at[k], target)

    sub, lane_at = iota((1, NH, W), 1), iota((1, NH, W), 2) // CO
    half_at = iota((48, W), 1) // CO
    lane_block = iota((48, 128), 1) // CO

    def fold(x):
        x = x[:, :128] + x[:, 128:]
        x = x + pltpu.roll(x, 64, 1)
        return x + pltpu.roll(x, 32, 1)

    comp[...] = jnp.zeros_like(comp)
    for a in range(3):
        own = acc[a * KM:(a + 1) * KM].reshape(48, NH, W)
        side = 3 * KM + a * 128
        for b in range(3):
            t = a * 3 + b
            diag = jnp.sum(jnp.where(sub == lane_at + (b - 1), own, 0.0), axis=1)
            if b == 0:
                diag = diag + jnp.where(half_at == 0, acc[side:side + 48], 0.0)
            if b == 2:
                diag = diag + jnp.where(half_at == NH - 1, acc[side + 48:side + 96], 0.0)
            diag = fold(diag)
            if t < 8:
                at = (t % 2) * 48
                comp[at:at + 48] += jnp.where(lane_block == t // 2, diag, 0.0)
            else:
                comp[96:128] += jnp.where(lane_block[:32] == 0, diag[:32], 0.0)
                comp[96:112] += jnp.where(lane_block[:16] == 1, diag[32:48], 0.0)
    comp[96:104] += jnp.where(lane_block[:8] == 2, fold(acc[3 * KM + 128 + ONES:3 * KM + 128 + ONES + 8]), 0.0)

    def scatter_copy(k):
        t, target = near_target(k)
        return remote(comp.at[pl.ds(pl.multiple_of(t * PIECE, PIECE), PIECE)], rs.at[near], s_a.at[k], r_a.at[k], target)

    def all_copy(k):
        return remote(piece, rs2.at[far], s_b.at[k], r_b.at[k], far_target(k)[1])

    own_piece = pl.ds(pl.multiple_of(near * PIECE, PIECE), PIECE)

    def gather_copy(k):
        here = full.at[own_piece]
        return remote(here, here, s_c.at[k], r_c.at[k], near_target(k)[1])

    pl.semaphore_wait(known.at[2], 2)
    run(NEAR, scatter_copy, "start")
    rs[near] = comp[own_piece]

    for q in range(PAIRS):
        total = cells[q]
        high = total.astype(BF)
        low = (total - high.astype(F32)).astype(BF)
        mean = dot(jnp.concatenate([high, low], axis=1), gather).astype(BF)
        ps[q] = dot(to_o_major, mean).astype(BF).reshape(CO, 4, 128)
    run(nh, pool_copy, "start")
    rpool[j] = ps[j]

    for d in range(ND):
        g = ga[d, ROWS:2 * ROWS]
        ga[d, 0:ROWS] = shift_left(g)
        ga[d, 2 * ROWS:3 * ROWS] = shift_right(g)

    def back(d):
        lo, hi = max(d - 1, 0), min(d + 2, ND)
        k0 = (lo - d + 1) * 3 * ROWS
        n = hi - lo
        return dot(tb[:, k0:k0 + n * 3 * ROWS], ga[lo:hi].reshape(n * 3 * ROWS, W))

    def keep(d, out):
        ph[0, d + 1] = out[XROWS:XROWS + CI].astype(BF)
        ph[1, d + 1] = out[XROWS + CI:].astype(BF)

    for side, d in ((0, -1), (1, ND)):
        out = back(d)
        pd[side] = out[:XROWS].astype(BF)
        keep(d, out)
    grad_copies = [
        remote(pd.at[0], rpd.at[1], s_g.at[0], r_g.at[0], (dn_i, j)),
        remote(pd.at[1], rpd.at[0], s_g.at[1], r_g.at[1], (up_i, j)),
        remote(ph.at[0, 0], rpc.at[1, 1], s_g.at[2], r_g.at[2], (dn_i, dn_j)),
        remote(ph.at[1, 0], rpc.at[1, 0], s_g.at[3], r_g.at[3], (dn_i, up_j)),
        remote(ph.at[0, ND + 1], rpc.at[0, 1], s_g.at[4], r_g.at[4], (up_i, dn_j)),
        remote(ph.at[1, ND + 1], rpc.at[0, 0], s_g.at[5], r_g.at[5], (up_i, up_j)),
    ]
    for copy in grad_copies:
        copy.start()

    def send_rows(n, d, count):
        for side, t in ((0, dn_j), (1, up_j)):
            at = 6 + 2 * n + side
            copy = remote(ph.at[side, pl.ds(d + 1, count)], rp.at[1 - side, pl.ds(d, count)],
                          s_g.at[at], r_g.at[at], (i, t))
            copy.start()
            grad_copies.append(copy)

    for d in (0, ND - 1):
        out = back(d)
        om[d] = out[:XROWS]
        keep(d, out)

    run(NEAR, scatter_copy, "wait_recv")
    total = rs[0]
    for k in range(1, NEAR):
        total = total + rs[k]
    piece[...] = total
    rs2[far] = total
    run(FAR, all_copy, "start")

    def inner(d0, count):
        def step(n, carry):
            for k in range(2):
                d = d0 + 2 * n + k
                out = dot(tb[...], ga[pl.ds(d - 1, 3)].reshape(9 * ROWS, W))
                om[d] = out[:XROWS]
                ph[0, d + 1] = out[XROWS:XROWS + CI].astype(BF)
                ph[1, d + 1] = out[XROWS + CI:].astype(BF)
            return carry
        lax.fori_loop(0, count // 2, step, 0)

    inner(1, 4)
    send_rows(0, 0, 5)
    inner(5, 4)
    send_rows(1, 5, 4)
    inner(9, 6)
    send_rows(2, 9, 7)

    run(FAR, all_copy, "wait_recv")
    total = rs2[0]
    for k in range(1, FAR):
        total = total + rs2[k]
    full[own_piece] = total
    run(NEAR, gather_copy, "start")

    run(nh, pool_copy, "wait_recv")
    for o in range(CO):
        pooled[o, 0] = rpool[:, o].reshape(4 * nh, 128)
    stores = [pltpu.make_async_copy(pooled, pooled_out, s_o.at[4])]
    stores[0].start()

    for copy in grad_copies:
        copy.wait_recv()
    row, col = iota((XROWS, 2 * CI), 0), iota((XROWS, 2 * CI), 1)
    place = one_hot(row == (col % CI) * NH + (col // CI) * (NH - 1))
    zero_rows = jnp.zeros((CI, W), BF)

    def edges(low, high, none):
        return dot(place, jnp.concatenate([jnp.where(first_j | none, zero_rows, low),
                                           jnp.where(last_j | none, zero_rows, high)], axis=0))

    for d in range(ND):
        out = om[d] + edges(rp[0, d], rp[1, d], False)
        if d in (0, ND - 1):
            side = 0 if d == 0 else 1
            none = first_i if d == 0 else last_i
            out = out + edges(rpc[side, 0], rpc[side, 1], none)
            out = out + jnp.where(none, zero_slab, rpd[side]).astype(F32)
        gvol[:, d] = out.astype(BF).reshape(CI, NH, W)
        if d % 4 == 3:
            part = pl.ds(d - 3, 4)
            stores.append(pltpu.make_async_copy(gvol.at[:, part], gvol_out.at[:, part], s_o.at[d // 4]))
            stores[-1].start()

    run(NEAR, gather_copy, "wait_recv")
    norm = 1.0 / math.sqrt(float(ND * NH * W * nd * nh))
    final = full[...] * norm
    turned = final.T
    for t in range(8):
        gker[t // 3, t % 3] = turned[(t // 2) * CO:(t // 2 + 1) * CO, (t % 2) * 48:(t % 2 + 1) * 48]
    gker[2, 2, :, 0:32] = turned[0:CO, 96:128]
    gker[2, 2, :, 32:48] = turned[CO:2 * CO, 96:112]
    gbias[...] = final[96:97, 2 * CO:3 * CO]

    for copy in stores:
        copy.wait()
    for copy in vol_copies + grad_copies:
        copy.wait_send()
    run(nh, pool_copy, "wait_send")
    run(NEAR, scatter_copy, "wait_send")
    run(FAR, all_copy, "wait_send")
    run(NEAR, gather_copy, "wait_send")


def hand_over(*refs):
    n = len(refs) // 2
    for k in range(n):
        refs[n + k][...] = refs[k][...]


def shards(nd, nh, volume, kernel, conv_bias, cotangent):
    vmem = pl.BlockSpec(memory_space=pltpu.VMEM)
    anywhere = pl.BlockSpec(memory_space=pl.ANY)
    dma = pltpu.SemaphoreType.DMA
    out_shape = (
        jax.ShapeDtypeStruct((CO, 1, 4 * nh, 128), BF),
        jax.ShapeDtypeStruct((CI, ND, NH, W), BF),
        jax.ShapeDtypeStruct((3, 3, CO, 3 * CI), F32),
        jax.ShapeDtypeStruct((1, CO), F32),
    )
    results = pl.pallas_call(
        functools.partial(kernel_body, nd, nh),
        out_shape=out_shape,
        in_specs=[anywhere, vmem, vmem, anywhere],
        out_specs=(anywhere, anywhere, vmem, vmem),
        scratch_shapes=[
            pltpu.VMEM((CI, ND, NH, W), BF),
            pltpu.VMEM((CO, PAIRS, 4, 128), BF),
            pltpu.VMEM((ND + 2, KM, W), BF),
            pltpu.VMEM((ND + 2, 128, W), BF),
            pltpu.VMEM((ND, 3 * ROWS, W), BF),
            pltpu.VMEM((ROWS, 3 * KM), BF),
            pltpu.VMEM((2 * CO, 3 * 128), BF),
            pltpu.VMEM((XROWS + 2 * CI, 9 * ROWS), BF),
            pltpu.VMEM((3 * KM + 3 * 128, ROWS), F32),
            pltpu.VMEM((ND, ROWS, W), F32),
            pltpu.VMEM((ND, XROWS, W), F32),
            pltpu.VMEM((PAIRS, 128, W), F32),
            pltpu.VMEM((PAIRS, 128, W), F32),
            pltpu.VMEM((2, ND, CI, W), BF),
            pltpu.VMEM((2, ND + 2, CI, W), BF),
            pltpu.VMEM((2, CI, NH, W), BF),
            pltpu.VMEM((PAIRS, CO, 4, 128), BF),
            pltpu.VMEM((PAIRS, CO, 4, 128), BF),
            pltpu.VMEM((2, ND + 2, CI, W), BF),
            pltpu.VMEM((2, ND, CI, W), BF),
            pltpu.VMEM((2, 2, CI, W), BF),
            pltpu.VMEM((2, XROWS, W), BF),
            pltpu.VMEM((2, XROWS, W), BF),
            pltpu.VMEM((128, 128), F32),
            pltpu.VMEM((NEAR, PIECE, 128), F32),
            pltpu.VMEM((FAR, PIECE, 128), F32),
            pltpu.VMEM((PIECE, 128), F32),
            pltpu.VMEM((128, 128), F32),
            pltpu.VMEM((CO, 1, 4 * nh, 128), BF),
            pltpu.VMEM((CI, ND, NH, W), BF),
            dma((2,)),
            dma((5,)),
            dma((8,)), dma((8,)),
            dma((nh,)), dma((nh,)),
            dma((12,)), dma((12,)),
            dma((NEAR,)), dma((NEAR,)),
            dma((FAR,)), dma((FAR,)),
            dma((NEAR,)), dma((NEAR,)),
            pltpu.SemaphoreType.REGULAR((3,)),
        ],
        compiler_params=pltpu.CompilerParams(
            collective_id=0, has_side_effects=True, vmem_limit_bytes=58 * 2**20),
        cost_estimate=pl.CostEstimate(flops=10 * 10**9, bytes_accessed=3 * 2**20, transcendentals=2 * 2**20),
        name="conv_step",
    )(volume, kernel.reshape(3, 3 * CO, 3 * CI), conv_bias.reshape(1, CO), cotangent)
    pooled, gvol, gker, gbias = pl.pallas_call(
        hand_over,
        out_shape=out_shape,
        in_specs=[vmem] * 4,
        out_specs=(vmem,) * 4,
        name="hand_over",
    )(*results)
    return pooled, gvol, gker, gbias.reshape(CO)


def solution(mesh):
    nd, nh = mesh.shape["depth"], mesh.shape["height"]
    in_specs = (P(None, "depth", "height", None), P(), P(), P(None, "depth", "height", None))
    out_specs = (
        P(None, ("depth", "height"), None, None),
        P(None, "depth", "height", None),
        P(),
        P(),
    )
    return jax.shard_map(
        functools.partial(shards, nd, nh), mesh=mesh, in_specs=in_specs, out_specs=out_specs, check_vma=False)
```

```python
import functools
import math

import jax
import jax.numpy as jnp
from jax import lax
from jax.experimental import pallas as pl
from jax.experimental.pallas import tpu as pltpu
from jax.sharding import PartitionSpec as P

BF = jnp.bfloat16
F32 = jnp.float32
MESH = pl.DeviceIdType.MESH

CI, CO, ND, NH, W = 16, 32, 16, 8, 256
ROWS = CO * NH
XROWS = CI * NH
KM = 3 * XROWS
ONES = 96
PAIRS = ND // 2
RING = 4
NEAR = 8
FAR = RING * RING
PIECE = 128 // NEAR


def dot(a, b):
    return jnp.dot(a, b, preferred_element_type=F32)


def dot_nt(a, b):
    return lax.dot_general(a, b, (((1,), (1,)), ((), ())), preferred_element_type=F32)


def iota(shape, dim):
    return lax.broadcasted_iota(jnp.int32, shape, dim)


def one_hot(cond, value=1.0):
    return jnp.where(cond, value, 0.0).astype(BF)


def shift_right(x):
    rolled = pltpu.roll(x, 1, 1)
    return jnp.where(iota(x.shape, 1) == 0, jnp.zeros_like(x), rolled)


def shift_left(x):
    rolled = pltpu.roll(x, x.shape[1] - 1, 1)
    return jnp.where(iota(x.shape, 1) == x.shape[1] - 1, jnp.zeros_like(x), rolled)


def in_fours(count, body):
    def step(n, carry):
        for k in range(4):
            body(4 * n + k)
        return carry
    lax.fori_loop(0, count // 4, step, 0)


def kernel_body(nd, nh, vol_in, ker, bias, cot_in, pooled_out, gvol_out, gker, gbias,
                vol, cot, xa, xh, ga, tm, th, tb, acc, bm, om, um, cells, hs, rh, rd, ps, rpool, ph, rp, rpc, pd, rpd, comp, rs, rs2, piece,
                full, pooled, gvol, s_in, s_o, s_v, r_v, s_p, r_p, s_g, r_g, s_a, r_a, s_b, r_b, s_c, r_c, known):
    i = lax.axis_index("depth")
    j = lax.axis_index("height")
    up_i, dn_i = lax.rem(i + 1, nd), lax.rem(i + nd - 1, nd)
    up_j, dn_j = lax.rem(j + 1, nh), lax.rem(j + nh - 1, nh)
    first_i, last_i = i == 0, i == nd - 1
    first_j, last_j = j == 0, j == nh - 1
    near = lax.rem(j, 2) * 4 + lax.rem(i, 4)
    far = (i // 4) * RING + j // 2

    def near_target(k):
        t = lax.rem(near + k, NEAR)
        return t, ((i // 4) * 4 + lax.rem(t, 4), (j // 2) * 2 + t // 4)

    def far_target(k):
        t = lax.rem(far + k, FAR)
        return t, ((t // RING) * 4 + lax.rem(i, 4), lax.rem(t, RING) * 2 + lax.rem(j, 2))

    def high_target(k):
        t = lax.rem(j + k, nh)
        return t, (i, t)

    vol_load = pltpu.make_async_copy(vol_in, vol, s_in.at[0])
    cot_load = pltpu.make_async_copy(cot_in, cot, s_in.at[1])
    vol_load.start()
    cot_load.start()
    barrier = pltpu.get_barrier_semaphore()

    def greet(sem, targets):
        for target in targets:
            pl.semaphore_signal(sem, inc=1, device_id=target, device_id_type=MESH)

    def around(n):
        at_i = (lax.rem(i + nd - n, nd), i, lax.rem(i + n, nd))
        at_j = (lax.rem(j + nh - n, nh), j, lax.rem(j + n, nh))
        return [(at_i[a], at_j[b]) for a in range(3) for b in range(3) if (a, b) != (1, 1)]

    greet(barrier, around(1))

    row, col = iota((2 * CI, XROWS), 0), iota((2 * CI, XROWS), 1)
    edge_rows = one_hot(col == (row % CI) * NH + (row // CI) * (NH - 1))
    vol_load.wait()
    for d in range(ND):
        edge = dot(edge_rows, vol[:, d].reshape(XROWS, W)).astype(BF)
        hs[0, d] = edge[:CI]
        hs[1, d] = edge[CI:]

    pl.semaphore_wait(barrier, 8)
    greet(known.at[0], around(1))

    def remote(src, dst, send, recv, target):
        return pltpu.make_async_remote_copy(
            src_ref=src, dst_ref=dst, send_sem=send, recv_sem=recv, device_id=target, device_id_type=MESH)

    vol_copies = [
        remote(vol.at[:, 0], rd.at[1], s_v.at[0], r_v.at[0], (dn_i, j)),
        remote(vol.at[:, ND - 1], rd.at[0], s_v.at[1], r_v.at[1], (up_i, j)),
        remote(hs.at[0, 0], rh.at[1, ND + 1], s_v.at[2], r_v.at[2], (dn_i, dn_j)),
        remote(hs.at[0, ND - 1], rh.at[1, 0], s_v.at[3], r_v.at[3], (up_i, dn_j)),
        remote(hs.at[1, 0], rh.at[0, ND + 1], s_v.at[4], r_v.at[4], (dn_i, up_j)),
        remote(hs.at[1, ND - 1], rh.at[0, 0], s_v.at[5], r_v.at[5], (up_i, up_j)),
        remote(hs.at[0], rh.at[1, pl.ds(1, ND)], s_v.at[6], r_v.at[6], (i, dn_j)),
        remote(hs.at[1], rh.at[0, pl.ds(1, ND)], s_v.at[7], r_v.at[7], (i, up_j)),
    ]
    for copy in vol_copies:
        copy.start()

    def put_slab(p, x):
        xa[p, 0:XROWS] = shift_right(x)
        xa[p, XROWS:2 * XROWS] = x
        xa[p, 2 * XROWS:3 * XROWS] = shift_left(x)

    for d in range(ND):
        put_slab(d + 1, vol[:, d].reshape(XROWS, W))

    row, col = iota((3 * CI, 640), 0), iota((3 * CI, 640), 1)
    expand = one_hot(((col < 384) & (row == col // NH))
                     | ((col >= 384) & (col < 512) & (row == col - 384))
                     | ((col >= 512) & (row + 3 * CI == col - 512)))
    lane_h = iota((CO, 384), 1) % NH
    for a in range(3):
        taps = dot(ker[a], expand)
        for h in range(NH):
            band = jnp.zeros((CO, 384), F32)
            for b in range(3):
                if 0 <= h + b - 1 < NH:
                    band = jnp.where(lane_h == h + b - 1, taps[b * CO:(b + 1) * CO, :384], band)
            tm[h * CO:(h + 1) * CO, a * KM:(a + 1) * KM] = band.astype(BF)
        th[0:CO, a * 128:(a + 1) * 128] = taps[0:CO, 384:512].astype(BF)
        th[CO:2 * CO, a * 128:(a + 1) * 128] = taps[2 * CO:3 * CO, 512:640].astype(BF)

    pl.semaphore_wait(known.at[0], 8)
    greet(known.at[1], around(2))

    def own_part(d):
        lo, hi = max(d, 1), min(d + 3, ND + 1)
        k0 = (lo - d) * KM
        bm[d] = dot(tm[:, k0:k0 + (hi - lo) * KM], xa[lo:hi].reshape((hi - lo) * KM, W))

    def own_parts(n, carry):
        for k in range(7):
            d = 1 + 7 * n + k
            bm[d] = dot(tm[...], xa[pl.ds(d, 3)].reshape(3 * KM, W))
        return carry

    lax.fori_loop(0, 2, own_parts, 0)
    own_part(0)
    own_part(ND - 1)

    row, col = iota((128, 128), 0), iota((128, 128), 1)
    to_h_major = one_hot(col == (row % CO) * 4 + row // CO)
    to_o_major = one_hot(col == (row % 4) * CO + row // 4)
    spread = one_hot(iota((128, W), 0) == iota((128, W), 1) // 2)
    gather = one_hot((iota((2 * W, 128), 0) % W) // 2 == iota((2 * W, 128), 1), 0.125)
    cot_load.wait()
    for q in range(PAIRS):
        ct = cot[:, q].reshape(128, 128)
        um[q] = dot(dot(to_h_major, ct).astype(BF), spread)
    eye = iota((CO, CO), 0) == iota((CO, CO), 1)
    bias_col = jnp.sum(jnp.where(eye, jnp.broadcast_to(bias[...], (CO, CO)), 0.0), axis=1, keepdims=True)
    bias_rows = jnp.concatenate([bias_col] * NH, axis=0)

    ones_rows = one_hot(iota((128 - ONES, W), 0) == 0)
    for p in range(ND + 2):
        xh[p, ONES:128] = ones_rows

    for a in range(3):
        flipped = tm[:, a * KM:(a + 1) * KM].T
        side = jnp.concatenate([th[0:CO, a * 128:(a + 1) * 128], jnp.zeros((ROWS - 2 * CO, 128), BF),
                                th[CO:2 * CO, a * 128:(a + 1) * 128]], axis=0).T
        for e in range(3):
            at = (2 - a) * 3 * ROWS + e * ROWS
            tb[0:XROWS, at:at + ROWS] = flipped[e * XROWS:(e + 1) * XROWS]
            tb[XROWS:XROWS + CI, at:at + ROWS] = side[e * CI:(e + 1) * CI]
            tb[XROWS + CI:XROWS + 2 * CI, at:at + ROWS] = side[48 + e * CI:48 + (e + 1) * CI]

    pl.semaphore_wait(known.at[1], 8)
    far_apart = [(lax.rem(i + 4, nd), j), (lax.rem(i + nd - 4, nd), j)]
    greet(known.at[2], far_apart)

    for copy in vol_copies:
        copy.wait_recv()
    zero_slab = jnp.zeros((XROWS, W), BF)
    put_slab(0, jnp.where(first_i, zero_slab, rd[0].reshape(XROWS, W)))
    put_slab(ND + 1, jnp.where(last_i, zero_slab, rd[1].reshape(XROWS, W)))
    for p in range(ND + 2):
        edge = first_i if p == 0 else last_i if p == ND + 1 else False
        for side, outside in ((0, first_j), (1, last_j)):
            x = jnp.where(outside | edge, jnp.zeros((CI, W), BF), rh[side, p])
            at = side * 48
            xh[p, at:at + CI] = shift_right(x)
            xh[p, at + CI:at + 2 * CI] = x
            xh[p, at + 2 * CI:at + 3 * CI] = shift_left(x)
    bm[0] += dot(tm[:, 0:KM], xa[0])
    bm[ND - 1] += dot(tm[:, 2 * KM:3 * KM], xa[ND + 1])

    def forward(q):
        total = None
        for k in range(2):
            d = 2 * q + k
            rim = dot(th[...], xh[d:d + 3].reshape(3 * 128, W))
            own = bm[d]
            before = jnp.concatenate([own[:CO] + rim[:CO], own[CO:ROWS - CO], own[ROWS - CO:] + rim[CO:]], axis=0)
            before = before + bias_rows
            t = jnp.tanh(0.5 * before)
            act = jnp.maximum(before, 0.3 * before) - 0.7 * jnp.log(0.5 + 0.5 * jnp.abs(t))
            slope = (0.08125 + 0.04375 * t).reshape(4, 2, CO, W)
            ga[d, ROWS:2 * ROWS] = (um[q].reshape(4, 1, CO, W) * slope).reshape(ROWS, W).astype(BF)
            part = act.reshape(4, 2, CO, W).sum(axis=1).reshape(128, W)
            total = part if total is None else total + part
        cells[q] = total

    def taps_grad(s):
        ds = [4 * s + k for k in range(4)]
        right = jnp.concatenate([ga[d, ROWS:2 * ROWS] for d in ds], axis=1)
        own = dot_nt(jnp.concatenate([xa[d:d + 3].reshape(3 * KM, W) for d in ds], axis=1), right)
        rim = dot_nt(jnp.concatenate([xh[d:d + 3].reshape(3 * 128, W) for d in ds], axis=1), right)
        if s == 0:
            acc[0:3 * KM] = own
            acc[3 * KM:] = rim
        else:
            acc[0:3 * KM] += own
            acc[3 * KM:] += rim

    stages = ND // 4
    for s in range(stages + 1):
        if s < stages:
            forward(2 * s)
            forward(2 * s + 1)
        if s > 0:
            taps_grad(s - 1)

    def run(count, make, act):
        def step(k, carry):
            getattr(make(k), act)()
            return carry
        lax.fori_loop(1, count, step, 0)

    def pool_copy(k):
        t, target = high_target(k)
        return remote(ps.at[t], rpool.at[j], s_p.at[k], r_p.at[k], target)

    sub, lane_at = iota((1, NH, W), 1), iota((1, NH, W), 2) // CO
    half_at = iota((48, W), 1) // CO
    lane_block = iota((48, 128), 1) // CO

    def fold(x):
        x = x[:, :128] + x[:, 128:]
        x = x + pltpu.roll(x, 64, 1)
        return x + pltpu.roll(x, 32, 1)

    comp[...] = jnp.zeros_like(comp)
    for a in range(3):
        own = acc[a * KM:(a + 1) * KM].reshape(48, NH, W)
        side = 3 * KM + a * 128
        for b in range(3):
            t = a * 3 + b
            diag = jnp.sum(jnp.where(sub == lane_at + (b - 1), own, 0.0), axis=1)
            if b == 0:
                diag = diag + jnp.where(half_at == 0, acc[side:side + 48], 0.0)
            if b == 2:
                diag = diag + jnp.where(half_at == NH - 1, acc[side + 48:side + 96], 0.0)
            diag = fold(diag)
            if t < 8:
                at = (t % 2) * 48
                comp[at:at + 48] += jnp.where(lane_block == t // 2, diag, 0.0)
            else:
                comp[96:128] += jnp.where(lane_block[:32] == 0, diag[:32], 0.0)
                comp[96:112] += jnp.where(lane_block[:16] == 1, diag[32:48], 0.0)
    comp[96:104] += jnp.where(lane_block[:8] == 2, fold(acc[3 * KM + 128 + ONES:3 * KM + 128 + ONES + 8]), 0.0)

    def scatter_copy(k):
        t, target = near_target(k)
        return remote(comp.at[pl.ds(pl.multiple_of(t * PIECE, PIECE), PIECE)], rs.at[near], s_a.at[k], r_a.at[k], target)

    def all_copy(k):
        return remote(piece, rs2.at[far], s_b.at[k], r_b.at[k], far_target(k)[1])

    own_piece = pl.ds(pl.multiple_of(near * PIECE, PIECE), PIECE)

    def gather_copy(k):
        here = full.at[own_piece]
        return remote(here, here, s_c.at[k], r_c.at[k], near_target(k)[1])

    pl.semaphore_wait(known.at[2], 2)
    run(NEAR, scatter_copy, "start")
    rs[near] = comp[own_piece]

    def pool(q):
        total = cells[q]
        high = total.astype(BF)
        low = (total - high.astype(F32)).astype(BF)
        mean = dot(jnp.concatenate([high, low], axis=1), gather).astype(BF)
        ps[q] = dot(to_o_major, mean).astype(BF).reshape(CO, 4, 128)

    in_fours(PAIRS, pool)
    run(nh, pool_copy, "start")
    rpool[j] = ps[j]

    def widen(d):
        g = ga[d, ROWS:2 * ROWS]
        ga[d, 0:ROWS] = shift_left(g)
        ga[d, 2 * ROWS:3 * ROWS] = shift_right(g)

    in_fours(ND, widen)

    run(NEAR, scatter_copy, "wait_recv")
    total = rs[0]
    for k in range(1, NEAR):
        total = total + rs[k]
    piece[...] = total
    rs2[far] = total
    run(FAR, all_copy, "start")

    def back(d):
        lo, hi = max(d - 1, 0), min(d + 2, ND)
        k0 = (lo - d + 1) * 3 * ROWS
        n = hi - lo
        return dot(tb[:, k0:k0 + n * 3 * ROWS], ga[lo:hi].reshape(n * 3 * ROWS, W))

    def keep(d, out):
        ph[0, d + 1] = out[XROWS:XROWS + CI].astype(BF)
        ph[1, d + 1] = out[XROWS + CI:].astype(BF)

    for side, d in ((0, -1), (1, ND)):
        out = back(d)
        pd[side] = out[:XROWS].astype(BF)
        keep(d, out)
    grad_copies = [
        remote(pd.at[0], rpd.at[1], s_g.at[0], r_g.at[0], (dn_i, j)),
        remote(pd.at[1], rpd.at[0], s_g.at[1], r_g.at[1], (up_i, j)),
        remote(ph.at[0, 0], rpc.at[1, 1], s_g.at[2], r_g.at[2], (dn_i, dn_j)),
        remote(ph.at[1, 0], rpc.at[1, 0], s_g.at[3], r_g.at[3], (dn_i, up_j)),
        remote(ph.at[0, ND + 1], rpc.at[0, 1], s_g.at[4], r_g.at[4], (up_i, dn_j)),
        remote(ph.at[1, ND + 1], rpc.at[0, 0], s_g.at[5], r_g.at[5], (up_i, up_j)),
    ]
    for copy in grad_copies:
        copy.start()

    def send_rows(n, d, count):
        for side, t in ((0, dn_j), (1, up_j)):
            at = 6 + 2 * n + side
            copy = remote(ph.at[side, pl.ds(d + 1, count)], rp.at[1 - side, pl.ds(d, count)],
                          s_g.at[at], r_g.at[at], (i, t))
            copy.start()
            grad_copies.append(copy)

    for d in (0, ND - 1):
        out = back(d)
        om[d] = out[:XROWS]
        keep(d, out)

    def inner(d0, count):
        def step(n, carry):
            for k in range(2):
                d = d0 + 2 * n + k
                out = dot(tb[...], ga[pl.ds(d - 1, 3)].reshape(9 * ROWS, W))
                om[d] = out[:XROWS]
                ph[0, d + 1] = out[XROWS:XROWS + CI].astype(BF)
                ph[1, d + 1] = out[XROWS + CI:].astype(BF)
            return carry
        lax.fori_loop(0, count // 2, step, 0)

    inner(1, 4)
    send_rows(0, 0, 5)
    inner(5, 4)
    send_rows(1, 5, 4)
    inner(9, 6)
    send_rows(2, 9, 7)

    run(FAR, all_copy, "wait_recv")
    total = rs2[0]
    for k in range(1, FAR):
        total = total + rs2[k]
    full[own_piece] = total
    run(NEAR, gather_copy, "start")

    run(nh, pool_copy, "wait_recv")
    for o in range(CO):
        pooled[o, 0] = rpool[:, o].reshape(4 * nh, 128)
    stores = [pltpu.make_async_copy(pooled, pooled_out, s_o.at[4])]
    stores[0].start()

    for copy in grad_copies:
        copy.wait_recv()
    row, col = iota((XROWS, 2 * CI), 0), iota((XROWS, 2 * CI), 1)
    place = one_hot(row == (col % CI) * NH + (col // CI) * (NH - 1))
    zero_rows = jnp.zeros((CI, W), BF)

    def edges(low, high, none):
        return dot(place, jnp.concatenate([jnp.where(first_j | none, zero_rows, low),
                                           jnp.where(last_j | none, zero_rows, high)], axis=0))

    for d in range(ND):
        out = om[d] + edges(rp[0, d], rp[1, d], False)
        if d in (0, ND - 1):
            side = 0 if d == 0 else 1
            none = first_i if d == 0 else last_i
            out = out + edges(rpc[side, 0], rpc[side, 1], none)
            out = out + jnp.where(none, zero_slab, rpd[side]).astype(F32)
        gvol[:, d] = out.astype(BF).reshape(CI, NH, W)
        if d % 4 == 3:
            part = pl.ds(d - 3, 4)
            stores.append(pltpu.make_async_copy(gvol.at[:, part], gvol_out.at[:, part], s_o.at[d // 4]))
            stores[-1].start()

    run(NEAR, gather_copy, "wait_recv")
    norm = 1.0 / math.sqrt(float(ND * NH * W * nd * nh))
    final = full[...] * norm
    turned = final.T
    for t in range(8):
        gker[t // 3, t % 3] = turned[(t // 2) * CO:(t // 2 + 1) * CO, (t % 2) * 48:(t % 2 + 1) * 48]
    gker[2, 2, :, 0:32] = turned[0:CO, 96:128]
    gker[2, 2, :, 32:48] = turned[CO:2 * CO, 96:112]
    gbias[...] = final[96:97, 2 * CO:3 * CO]

    for copy in stores:
        copy.wait()
    for copy in vol_copies + grad_copies:
        copy.wait_send()
    run(nh, pool_copy, "wait_send")
    run(NEAR, scatter_copy, "wait_send")
    run(FAR, all_copy, "wait_send")
    run(NEAR, gather_copy, "wait_send")


def hand_over(*refs):
    n = len(refs) // 2
    for k in range(n):
        refs[n + k][...] = refs[k][...]


def shards(nd, nh, volume, kernel, conv_bias, cotangent):
    vmem = pl.BlockSpec(memory_space=pltpu.VMEM)
    anywhere = pl.BlockSpec(memory_space=pl.ANY)
    dma = pltpu.SemaphoreType.DMA
    out_shape = (
        jax.ShapeDtypeStruct((CO, 1, 4 * nh, 128), BF),
        jax.ShapeDtypeStruct((CI, ND, NH, W), BF),
        jax.ShapeDtypeStruct((3, 3, CO, 3 * CI), F32),
        jax.ShapeDtypeStruct((1, CO), F32),
    )
    results = pl.pallas_call(
        functools.partial(kernel_body, nd, nh),
        out_shape=out_shape,
        in_specs=[anywhere, vmem, vmem, anywhere],
        out_specs=(anywhere, anywhere, vmem, vmem),
        scratch_shapes=[
            pltpu.VMEM((CI, ND, NH, W), BF),
            pltpu.VMEM((CO, PAIRS, 4, 128), BF),
            pltpu.VMEM((ND + 2, KM, W), BF),
            pltpu.VMEM((ND + 2, 128, W), BF),
            pltpu.VMEM((ND, 3 * ROWS, W), BF),
            pltpu.VMEM((ROWS, 3 * KM), BF),
            pltpu.VMEM((2 * CO, 3 * 128), BF),
            pltpu.VMEM((XROWS + 2 * CI, 9 * ROWS), BF),
            pltpu.VMEM((3 * KM + 3 * 128, ROWS), F32),
            pltpu.VMEM((ND, ROWS, W), F32),
            pltpu.VMEM((ND, XROWS, W), F32),
            pltpu.VMEM((PAIRS, 128, W), F32),
            pltpu.VMEM((PAIRS, 128, W), F32),
            pltpu.VMEM((2, ND, CI, W), BF),
            pltpu.VMEM((2, ND + 2, CI, W), BF),
            pltpu.VMEM((2, CI, NH, W), BF),
            pltpu.VMEM((PAIRS, CO, 4, 128), BF),
            pltpu.VMEM((PAIRS, CO, 4, 128), BF),
            pltpu.VMEM((2, ND + 2, CI, W), BF),
            pltpu.VMEM((2, ND, CI, W), BF),
            pltpu.VMEM((2, 2, CI, W), BF),
            pltpu.VMEM((2, XROWS, W), BF),
            pltpu.VMEM((2, XROWS, W), BF),
            pltpu.VMEM((128, 128), F32),
            pltpu.VMEM((NEAR, PIECE, 128), F32),
            pltpu.VMEM((FAR, PIECE, 128), F32),
            pltpu.VMEM((PIECE, 128), F32),
            pltpu.VMEM((128, 128), F32),
            pltpu.VMEM((CO, 1, 4 * nh, 128), BF),
            pltpu.VMEM((CI, ND, NH, W), BF),
            dma((2,)),
            dma((5,)),
            dma((8,)), dma((8,)),
            dma((nh,)), dma((nh,)),
            dma((12,)), dma((12,)),
            dma((NEAR,)), dma((NEAR,)),
            dma((FAR,)), dma((FAR,)),
            dma((NEAR,)), dma((NEAR,)),
            pltpu.SemaphoreType.REGULAR((3,)),
        ],
        compiler_params=pltpu.CompilerParams(
            collective_id=0, has_side_effects=True, vmem_limit_bytes=58 * 2**20),
        cost_estimate=pl.CostEstimate(flops=10 * 10**9, bytes_accessed=3 * 2**20, transcendentals=2 * 2**20),
        name="conv_step",
    )(volume, kernel.reshape(3, 3 * CO, 3 * CI), conv_bias.reshape(1, CO), cotangent)
    pooled, gvol, gker, gbias = pl.pallas_call(
        hand_over,
        out_shape=out_shape,
        in_specs=[vmem] * 4,
        out_specs=(vmem,) * 4,
        name="hand_over",
    )(*results)
    return pooled, gvol, gker, gbias.reshape(CO)


def solution(mesh):
    nd, nh = mesh.shape["depth"], mesh.shape["height"]
    in_specs = (P(None, "depth", "height", None), P(), P(), P(None, "depth", "height", None))
    out_specs = (
        P(None, ("depth", "height"), None, None),
        P(None, "depth", "height", None),
        P(),
        P(),
    )
    return jax.shard_map(
        functools.partial(shards, nd, nh), mesh=mesh, in_specs=in_specs, out_specs=out_specs, check_vma=False)
```
